128 devices in a mesh: sweep: 16 (over z, x), cross: 8 (over y, core).
Axes of the slice: x: 4, y: 4, z: 4, core: 2. Of those that a mesh axis runs over, the one named last changes fastest.
Arguments:
- old_state: float32 [20, 768, 2048], P(None, 'sweep', 'cross'), may hold values from -6 to 6
- offsets: float32 [2, 768, 2048], P(None, 'sweep', 'cross'), may hold values from -0.5 to 0.5
- limiter_flags: int32 [768, 2048], P('sweep', 'cross'), may hold values 0 or 1
- self_tiles: float32 [12288, 128, 128], P(('sweep', 'cross')), as said below
- flux_tiles: float32 [24576, 128, 128], P(('sweep', 'cross')), as said below
- tile_source: int32 [24576], P(('sweep', 'cross')), may hold values from 0 to 95
- tile_dest: int32 [24576, 1], P(('sweep', 'cross')), may hold values from 0 to 15; in each aligned block of 192 rows (0 to 191, 192 to 383, ...) at most 24 rows name the same one
- tile_target: int32 [24576], P(('sweep', 'cross')), may hold values from 0 to 95
Outputs:
- new_state: float32 [20, 768, 2048], P(None, 'sweep', 'cross')
The draws below stay inside these ranges and needn't reach their ends.
Inputs may be any that keep to these rules, and one draw needn't show every extreme that they name: A tile goes to the device of sweep index tile_dest with the sender's cross index. The tiles of one device name one sweep index at most 24 times, and in some devices exactly 24 times. `self_tiles`: entries are positive. `flux_tiles`: entries are positive.
All inputs are finite; a program needn't handle non-finite values. No bound on the sum of `limiter_flags` on one device may be relied on, other than what follows from the above.
Results may differ from the reference program's by a relative error of at most 0.0003.
Values sent between devices are 32-bit elements; how exact they have to be, the bound alone decides.
No kernel may reach another device: no remote copies, remote signals or barrier semaphores. Data moves between devices by JAX's collectives and lax.ppermute only.
A program may use at most 128 MiB of HBM per device.

```python
import math
import jax
import jax.numpy as jnp
import numpy as np
from jax import lax

F = 20
BLK = 128
ROWS = 48
COLS = 256
NB = 96
NT = 192
CAP = 24
TILES = 24576
NS = 768
NC = 2048
N_SWEEP = 16
N_CROSS = 8


def draw_self_tiles(key, part):
    key = jax.random.fold_in(key, 11)
    spread = jax.random.uniform(key, (N_SWEEP * N_CROSS * NB, BLK, BLK), jnp.float32, 0.05 / BLK, 1.0 / BLK)
    return spread + 0.5 * jnp.eye(BLK, dtype=jnp.float32)[None]


def draw_flux_tiles(key, part):
    key = jax.random.fold_in(key, 23)
    return jax.random.uniform(key, (TILES, BLK, BLK), jnp.float32, 0.05 / BLK, 1.0 / BLK)


def touch_ends(values, stream_key, low, top_value):
    shape = values.shape
    index_at = [jax.random.randint(jax.random.fold_in(stream_key, axis), (), 0, shape[axis]) for axis in range(len(shape))]
    values = values.at[tuple(index_at)].set(low)
    longest = shape.index(max(shape))
    index_at[longest] = (index_at[longest] + 1) % shape[longest]
    return values.at[tuple(index_at)].set(top_value)


def shard_levels(rng, shape, cuts, smallest, high):
    level = 1.0
    for position, shards_of in cuts:
        steps = jax.random.uniform(jax.random.fold_in(jax.random.fold_in(rng, 6), position), (shards_of,), jnp.float32, smallest / len(cuts), high / len(cuts))
        level = level * jnp.repeat(jnp.exp(steps), shape[position] // shards_of).reshape((-1,) + (1,) * (len(shape) - 1 - position))
    return level


def shared_out(rng, own, number, rows, count, top, reach, skew):
    sequence = jax.random.permutation(rng, count)
    crowded, usual = shares(count, rows * top, reach, skew, True), shares(count, rows * top, reach, skew, False)
    places = jnp.arange(count)

    def named(lengths, offset_by):
        used = int((lengths > 0).sum())
        fixed = max(1, used // 4)
        moved = fixed + (places - fixed + offset_by * (used - fixed)) % max(1, count - fixed)
        return jnp.zeros((count,), jnp.int32).at[sequence[jnp.where(places < fixed, places, moved)]].set(jnp.asarray(lengths, jnp.int32))

    lengths = jnp.where(number % 4 == 0, named(crowded, number // 4), named(usual, number - number // 4 - 1))
    mixed = jax.random.permutation(jax.random.fold_in(own, 3), count)
    donor, sink = mixed[0:count // 2 * 2:2], mixed[1:count // 2 * 2:2]
    slack = jnp.minimum(lengths[donor] - 1, reach - lengths[sink]) // 2
    slack = jnp.where((donor == sequence[0]) | (sink == sequence[0]) | (lengths[sink] == 0), 0, jnp.maximum(slack, 0))
    moved = jax.random.randint(jax.random.fold_in(own, 4), (count // 2,), 0, 1 << 20) % (slack + 1)
    lengths = lengths.at[donor].add(-moved).at[sink].add(moved)
    members = jnp.searchsorted(jnp.cumsum(lengths), jnp.arange(rows * top), side="right").astype(jnp.int32)
    listing = members.reshape(top, rows).T
    listing = listing[jax.random.permutation(jax.random.fold_in(own, 1), rows)]
    offset_by = jax.random.randint(jax.random.fold_in(own, 2), (rows, 1), 0, top)
    return jnp.take_along_axis(listing, (jnp.arange(top)[None, :] + offset_by) % top, axis=1)


def shares(number_of, total, most, slope, full):
    portions = [(1 << 20) // math.isqrt(grade ** slope) + 1 for grade in range(1, number_of + 1)]
    largest = most if full else min(most, max(-(-total // number_of), total * portions[0] // sum(portions)))
    least = 1 if total - largest >= number_of - 1 else 0
    given, surplus = [largest] + [least] * (number_of - 1), total - largest - least * (number_of - 1)
    while surplus > 0:
        candidates = [i for i in range(1, number_of) if given[i] < largest] or [i for i in range(1, number_of) if given[i] < most]
        pool, remaining = sum([portions[i] for i in candidates]), surplus
        for i in candidates:
            more = min(most - given[i], max(1, remaining * portions[i] // pool), surplus)
            given[i] = given[i] + more
            surplus = surplus - more
    return np.array(given)


def noise(stream_key, extent, width, reach, cuts=(), held_as=jnp.bfloat16):
    factor_of = shard_levels(stream_key, extent, cuts, -0.22, 0.18) if cuts else 1.0
    entries = jax.random.normal(stream_key, extent, jnp.float32) * width * factor_of
    return jnp.minimum(jnp.maximum(entries, -reach), reach).astype(held_as)


def setup_inputs(seed: int = 0) -> dict:
    key_list = jax.random.split(jax.random.key(seed), 9)
    old_state = noise(key_list[0], (F, NS, NC), 1.0, 6.0, ((1, 16), (2, 8)), jnp.float32)
    offsets = jnp.clip(jax.random.uniform(key_list[1], (2, NS, NC), jnp.float32, -0.5, 0.5) * shard_levels(key_list[1], (2, NS, NC), ((1, 16), (2, 8)), -0.4, 0.0), -0.5, 0.5)
    limiter_flags = touch_ends((jax.random.randint(key_list[2], (NS, NC), 0, 2) < 1).astype(jnp.int32), jax.random.fold_in(key_list[2], 1), 0, 1)
    self_tiles = draw_self_tiles(jax.random.fold_in(key_list[8], 71), 0)
    flux_tiles = draw_flux_tiles(jax.random.fold_in(key_list[8], 71), 0)
    tile_source = touch_ends(jax.random.randint(key_list[5], (TILES,), 0, NB), jax.random.fold_in(key_list[5], 1), 0, NB - 1).astype(jnp.int32)
    tile_dest_keys = jax.random.split(jax.random.fold_in(key_list[6], 1), TILES // NT)
    tile_dest_turns = jax.random.permutation(jax.random.fold_in(key_list[6], 3), TILES // NT)
    tile_dest = jax.vmap(lambda own, number: shared_out(jax.random.fold_in(key_list[6], 2), own, number, NT, N_SWEEP, 1, CAP, 2))(tile_dest_keys, tile_dest_turns).reshape((TILES, 1))
    tile_target = touch_ends(jax.random.randint(key_list[7], (TILES,), 0, NB), jax.random.fold_in(key_list[7], 1), 0, NB - 1).astype(jnp.int32)
    return dict(old_state=old_state, offsets=offsets, limiter_flags=limiter_flags, self_tiles=self_tiles, flux_tiles=flux_tiles, tile_source=tile_source, tile_dest=tile_dest, tile_target=tile_target)


SMOOTHING = 0.1


def slopes(padded, centre, limiter_flags, direction):
    if direction == 1:
        lower_cells = padded[:, :-2, 1:-1]
        upper_cells = padded[:, 2:, 1:-1]
    else:
        lower_cells = padded[:, 1:-1, :-2]
        upper_cells = padded[:, 1:-1, 2:]
    back_diff = centre - lower_cells
    front_diff = upper_cells - centre
    limited = 0.5 * (jnp.sign(back_diff) + jnp.sign(front_diff)) * jnp.minimum(jnp.abs(back_diff), jnp.abs(front_diff))
    return jnp.where(limiter_flags[None] > 0, limited, 0.5 * (back_diff + front_diff))


def reconstruct(padded, centre, offsets, limiter_flags):
    along = slopes(padded, centre, limiter_flags, 1)
    across = slopes(padded, centre, limiter_flags, 2)
    return centre + along * offsets[0][None] + across * offsets[1][None]


def smooth(padded, centre):
    beside_all = padded[:, :-2, 1:-1] + padded[:, 2:, 1:-1] + padded[:, 1:-1, :-2] + padded[:, 1:-1, 2:]
    return centre + SMOOTHING * (beside_all - 4.0 * centre)


def reference(old_state, offsets, limiter_flags, self_tiles, flux_tiles, tile_source, tile_dest, tile_target):
    highest = lax.Precision.HIGHEST
    padded = jnp.pad(old_state, ((0, 0), (1, 1), (1, 1)))
    rebuilt = reconstruct(padded, old_state, offsets, limiter_flags)
    devices = N_SWEEP * N_CROSS
    per_row = COLS // BLK
    blocks = rebuilt.reshape(F, N_SWEEP, ROWS, N_CROSS, per_row, BLK).transpose(1, 3, 2, 4, 0, 5).reshape(devices, NB, F, BLK)
    self_all = self_tiles.reshape(devices, NB, BLK, BLK)
    new_mass = jnp.einsum('dbpe,dbfe->dbfp', self_all, blocks, precision=highest)
    volume = jnp.sum(self_all, axis=3)
    sender = (jnp.arange(TILES) // NT).astype(jnp.int32)
    chosen = blocks[sender, tile_source.astype(jnp.int32)]
    contrib = jnp.einsum('tpe,tfe->tfp', flux_tiles, chosen, precision=highest)
    flux_volume = jnp.sum(flux_tiles, axis=2)
    receiver = (tile_dest[:, 0] * N_CROSS + sender % N_CROSS).astype(jnp.int32)
    target = tile_target.astype(jnp.int32)
    new_mass = new_mass.at[receiver, target].add(contrib)
    volume = volume.at[receiver, target].add(flux_volume)
    density = new_mass / volume[:, :, None, :]
    density = density.reshape(N_SWEEP, N_CROSS, ROWS, per_row, F, BLK).transpose(4, 0, 2, 1, 3, 5).reshape(F, NS, NC)
    padded_new = jnp.pad(density, ((0, 0), (1, 1), (1, 1)))
    return smooth(padded_new, density)
```

```python
import functools

import jax
import jax.numpy as jnp
from jax import lax
from jax.experimental import pallas as pl
from jax.experimental.pallas import tpu as pltpu
from jax.sharding import PartitionSpec as P

SMOOTHING = 0.1
FIELDS, ROWS, COLS = 20, 48, 256
BLOCKS, BLK = 96, 128
TILES, CAP = 192, 24
SWEEPS, CROSSES = 16, 8
PAD = 24
WIDE = FIELDS + 1
SLOT_ROWS = CAP * WIDE
PART_ROWS = SLOT_ROWS + 8
CHUNK = 24
VMEM = pltpu.VMEM
SMEM = pltpu.SMEM
LIMIT = 60 * 1024 * 1024


def pairs(count, shift):
    out = []
    for i in range(count):
        j = ((i + shift) ^ 1) - shift
        if 0 <= j < count:
            out.append((i, j))
    return out


def swap(values, axis, shift):
    return lax.ppermute(values, axis, pairs(lax.axis_size(axis), shift))


def lane_of(shape):
    return lax.broadcasted_iota(jnp.int32, shape, len(shape) - 1)


def row_of(shape):
    return lax.broadcasted_iota(jnp.int32, shape, len(shape) - 2)


def column(ref, lane):
    lanes = lane_of((ROWS, BLK))
    packed = jnp.zeros((ROWS, BLK), jnp.float32)
    for f in range(FIELDS):
        packed = jnp.where(lanes == f, ref[f, :, lane : lane + 1], packed)
    return packed


def pack_edges(ref, sweep_odd, cross_odd, near_row, far_row, near_col, far_col):
    low, high = ref[:, 0, :], ref[:, ROWS - 1, :]
    near_row[...] = jnp.where(sweep_odd, low, high)
    far_row[...] = jnp.where(sweep_odd, high, low)
    low, high = column(ref, 0), column(ref, COLS - 1)
    near_col[...] = jnp.where(cross_odd, low, high)
    far_col[...] = jnp.where(cross_odd, high, low)


def edges_kernel(parity, ref, near_row, far_row, near_col, far_col):
    pack_edges(ref, parity[0] == 1, parity[1] == 1, near_row, far_row, near_col, far_col)


EDGES = (
    jax.ShapeDtypeStruct((FIELDS, COLS), jnp.float32),
    jax.ShapeDtypeStruct((FIELDS, COLS), jnp.float32),
    jax.ShapeDtypeStruct((ROWS, BLK), jnp.float32),
    jax.ShapeDtypeStruct((ROWS, BLK), jnp.float32),
)


def exchange(near_row, far_row, near_col, far_col):
    return (
        swap(near_row, "sweep", 0),
        swap(far_row, "sweep", 1),
        swap(near_col, "cross", 0),
        swap(far_col, "cross", 1),
    )


def neighbours(u, f, sweep_odd, cross_odd, halos):
    near_row, far_row, near_col, far_col = halos
    near, far = near_row[f : f + 1, :], far_row[f : f + 1, :]
    low_row = jnp.where(sweep_odd, near, far)
    high_row = jnp.where(sweep_odd, far, near)
    near, far = near_col[:, f : f + 1], far_col[:, f : f + 1]
    low_col = jnp.where(cross_odd, near, far)
    high_col = jnp.where(cross_odd, far, near)
    rows, lanes = row_of((ROWS, COLS)), lane_of((ROWS, COLS))
    up = jnp.where(rows == 0, low_row, pltpu.roll(u, 1, 0))
    down = jnp.where(rows == ROWS - 1, high_row, pltpu.roll(u, ROWS - 1, 0))
    left = jnp.where(lanes == 0, low_col, pltpu.roll(u, 1, 1))
    right = jnp.where(lanes == COLS - 1, high_col, pltpu.roll(u, COLS - 1, 1))
    return up, down, left, right


def slope(before, centre, after, limited):
    back, front = centre - before, after - centre
    least = jnp.maximum(jnp.minimum(back, front), 0.0) + jnp.minimum(jnp.maximum(back, front), 0.0)
    return jnp.where(limited, least, 0.5 * (back + front))


def split_dot(x, tile):
    tile_high = tile.astype(jnp.bfloat16)
    tile_low = (tile - tile_high.astype(jnp.float32)).astype(jnp.bfloat16)
    x_high = x.astype(jnp.bfloat16).astype(jnp.float32)
    x_low = x - x_high
    left = jnp.concatenate([x_high, x_low], axis=0).astype(jnp.bfloat16)
    right = jnp.concatenate([x_high, jnp.zeros_like(x)], axis=0).astype(jnp.bfloat16)
    moving = jnp.concatenate([left, right], axis=1)
    held = jnp.concatenate([tile_high, tile_low], axis=1)
    out = lax.dot_general(
        moving, held, (((1,), (1,)), ((), ())), preferred_element_type=jnp.float32
    )
    return out[:PAD] + out[PAD:]


def flux_kernel(
    parity, source, dest, target, old, offsets, flags, near_row, far_row, near_col, far_col,
    flux, send, blocks_out, x, tiles, sems, count,
):
    copies = [
        pltpu.make_async_copy(
            flux.at[pl.ds(c * CHUNK, CHUNK)], tiles.at[pl.ds(c * CHUNK, CHUNK)], sems.at[c]
        )
        for c in range(TILES // CHUNK)
    ]
    for copy in copies:
        copy.start()
    sweep_odd, cross_odd = parity[0] == 1, parity[1] == 1
    halos = (near_row, far_row, near_col, far_col)
    limited = flags[...] > 0
    for f in range(FIELDS):
        u = old[f]
        up, down, left, right = neighbours(u, f, sweep_odd, cross_odd, halos)
        rebuilt = (
            u
            + slope(up, u, down, limited) * offsets[0]
            + slope(left, u, right, limited) * offsets[1]
        )
        x[pl.ds(f, ROWS, stride=2 * PAD), :] = rebuilt[:, :BLK]
        x[pl.ds(PAD + f, ROWS, stride=2 * PAD), :] = rebuilt[:, BLK:]
    for f in range(FIELDS, PAD):
        x[pl.ds(f, BLOCKS, stride=PAD), :] = jnp.full(
            (BLOCKS, BLK), 1.0 if f == FIELDS else 0.0, jnp.float32
        )
    blocks_out[...] = x[...]
    for d in range(SWEEPS):
        count[d] = 0
        send[d, pl.ds(SLOT_ROWS, 8), :] = jnp.full((8, BLK), -1.0, jnp.float32)
    lanes = lane_of((1, BLK))

    for c in range(TILES // CHUNK):
        copies[c].wait()

        def step(k, carry):
            t = c * CHUNK + k
            d = dest[t]
            r = count[d]
            count[d] = r + 1
            out = split_dot(x[pl.ds(pl.multiple_of(source[t] * PAD, 8), PAD), :], tiles[t])
            send[d, pl.ds(r * WIDE, WIDE), :] = out[:WIDE]
            marks = send[d, pl.ds(SLOT_ROWS, 1), :]
            send[d, pl.ds(SLOT_ROWS, 1), :] = jnp.where(
                lanes == r, target[t].astype(jnp.float32), marks
            )
            return carry

        lax.fori_loop(0, CHUNK, step, 0, unroll=4)


def self_kernel(x, tiles, out):
    def step(k, carry):
        out[k] = split_dot(x[k], tiles[k])
        return carry

    lax.fori_loop(0, tiles.shape[0], step, 0, unroll=4)


def receive_kernel(
    parity, arrived, mass, density, near_row, far_row, near_col, far_col, total, marks, where, sem
):
    s = pl.program_id(0)

    @pl.when(s == 0)
    def _():
        total[...] = mass[...]

    marks[...] = jnp.broadcast_to(arrived[0, pl.ds(SLOT_ROWS, 1), :], (8, BLK)).astype(jnp.int32)
    copy = pltpu.make_async_copy(marks, where, sem)
    copy.start()
    copy.wait()

    def step(k, carry):
        b = where[0, k]

        @pl.when(b >= 0)
        def _():
            at = pl.ds(pl.multiple_of(b * PAD, 8), PAD)
            total[at, :] += arrived[0, pl.ds(k * WIDE, PAD), :]

        return carry

    lax.fori_loop(0, CAP, step, 0)

    @pl.when(s == SWEEPS - 1)
    def _():
        for f in range(FIELDS):
            halves = []
            for h in range(2):
                value = total[pl.ds(h * PAD + f, ROWS, stride=2 * PAD), :]
                volume = total[pl.ds(h * PAD + FIELDS, ROWS, stride=2 * PAD), :]
                halves.append(value / volume)
            density[f, :, :BLK] = halves[0]
            density[f, :, BLK:] = halves[1]
        pack_edges(density, parity[0] == 1, parity[1] == 1, near_row, far_row, near_col, far_col)


def smooth_kernel(parity, density, near_row, far_row, near_col, far_col, out):
    halos = (near_row, far_row, near_col, far_col)
    for f in range(FIELDS):
        u = density[f]
        up, down, left, right = neighbours(u, f, parity[0] == 1, parity[1] == 1, halos)
        out[f] = u + SMOOTHING * (up + down + left + right - 4.0 * u)


def params(**more):
    return pltpu.CompilerParams(vmem_limit_bytes=LIMIT, **more)


def body(
    old_state, offsets, limiter_flags, self_tiles, flux_tiles, tile_source, tile_dest, tile_target
):
    parity = jnp.stack([lax.axis_index("sweep") % 2, lax.axis_index("cross") % 2]).astype(jnp.int32)
    vm, sm, hbm = (pl.BlockSpec(memory_space=m) for m in (VMEM, SMEM, pl.ANY))
    edges = pl.pallas_call(
        edges_kernel, out_shape=EDGES, in_specs=[sm, vm], out_specs=(vm,) * 4,
        compiler_params=params(), name="edges",
    )(parity, old_state)
    halos = exchange(*edges)
    send, blocks = pl.pallas_call(
        flux_kernel,
        out_shape=(
            jax.ShapeDtypeStruct((SWEEPS, PART_ROWS, BLK), jnp.float32),
            jax.ShapeDtypeStruct((BLOCKS * PAD, BLK), jnp.float32),
        ),
        in_specs=[sm] * 4 + [vm] * 7 + [hbm],
        out_specs=(vm, vm),
        scratch_shapes=[
            VMEM((BLOCKS * PAD, BLK), jnp.float32),
            VMEM((TILES, BLK, BLK), jnp.float32),
            pltpu.SemaphoreType.DMA((TILES // CHUNK,)),
            SMEM((SWEEPS,), jnp.int32),
        ],
        compiler_params=params(),
        cost_estimate=pl.CostEstimate(
            flops=2 * 6 * TILES * PAD * BLK * BLK, bytes_accessed=TILES * BLK * BLK * 4, transcendentals=0
        ),
        name="flux",
    )(
        parity, tile_source, tile_dest.reshape(TILES), tile_target, old_state, offsets, limiter_flags,
        *halos, flux_tiles,
    )
    arrived = lax.all_to_all(send, "sweep", split_axis=0, concat_axis=0, tiled=True)
    step = 16
    mass = pl.pallas_call(
        self_kernel,
        grid=(BLOCKS // step,),
        out_shape=jax.ShapeDtypeStruct((BLOCKS, PAD, BLK), jnp.float32),
        in_specs=[
            pl.BlockSpec((step, PAD, BLK), lambda i: (i, 0, 0)),
            pl.BlockSpec((step, BLK, BLK), lambda i: (i, 0, 0)),
        ],
        out_specs=pl.BlockSpec((step, PAD, BLK), lambda i: (i, 0, 0)),
        compiler_params=params(),
        cost_estimate=pl.CostEstimate(
            flops=2 * 6 * BLOCKS * PAD * BLK * BLK, bytes_accessed=BLOCKS * BLK * BLK * 4, transcendentals=0
        ),
        name="own",
    )(blocks.reshape(BLOCKS, PAD, BLK), self_tiles)
    whole = lambda *shape: pl.BlockSpec(shape, lambda i: (0,) * len(shape))
    density, *edges = pl.pallas_call(
        receive_kernel,
        grid=(SWEEPS,),
        out_shape=(jax.ShapeDtypeStruct((FIELDS, ROWS, COLS), jnp.float32),) + EDGES,
        in_specs=[
            sm,
            pl.BlockSpec((1, PART_ROWS, BLK), lambda i: (i, 0, 0)),
            whole(BLOCKS * PAD, BLK),
        ],
        out_specs=(
            whole(FIELDS, ROWS, COLS), whole(FIELDS, COLS), whole(FIELDS, COLS),
            whole(ROWS, BLK), whole(ROWS, BLK),
        ),
        scratch_shapes=[
            VMEM((BLOCKS * PAD, BLK), jnp.float32),
            VMEM((8, BLK), jnp.int32),
            SMEM((8, BLK), jnp.int32),
            pltpu.SemaphoreType.DMA,
        ],
        compiler_params=params(),
        name="receive",
    )(parity, arrived, mass.reshape(BLOCKS * PAD, BLK))
    halos = exchange(*edges)
    return pl.pallas_call(
        smooth_kernel,
        out_shape=jax.ShapeDtypeStruct((FIELDS, ROWS, COLS), jnp.float32),
        in_specs=[sm] + [vm] * 5,
        out_specs=vm,
        compiler_params=params(),
        name="smooth",
    )(parity, density, *halos)


def solution(mesh):
    placed = (
        P(None, "sweep", "cross"),
        P(None, "sweep", "cross"),
        P("sweep", "cross"),
        P(("sweep", "cross"), None, None),
        P(("sweep", "cross"), None, None),
        P(("sweep", "cross")),
        P(("sweep", "cross"), None),
        P(("sweep", "cross")),
    )
    return jax.shard_map(
        body, mesh=mesh, in_specs=placed, out_specs=P(None, "sweep", "cross"), check_vma=False
    )
```

```python
import functools

import jax
import jax.numpy as jnp
from jax import lax
from jax.experimental import pallas as pl
from jax.experimental.pallas import tpu as pltpu
from jax.sharding import PartitionSpec as P

SMOOTHING = 0.1
FIELDS, ROWS, COLS = 20, 48, 256
BLOCKS, BLK = 96, 128
TILES, CAP = 192, 24
SWEEPS, CROSSES = 16, 8
PAD = 24
WIDE = FIELDS + 1
SLOT_ROWS = CAP * WIDE
PART_ROWS = SLOT_ROWS + 8
CHUNK = 24
VMEM = pltpu.VMEM
SMEM = pltpu.SMEM


def pairs(count, shift):
    out = []
    for i in range(count):
        j = ((i + shift) ^ 1) - shift
        if 0 <= j < count:
            out.append((i, j))
    return out


def swap(values, axis, shift):
    return lax.ppermute(values, axis, pairs(lax.axis_size(axis), shift))


def lane_of(shape):
    return lax.broadcasted_iota(jnp.int32, shape, len(shape) - 1)


def row_of(shape):
    return lax.broadcasted_iota(jnp.int32, shape, len(shape) - 2)


def column(ref, lane):
    lanes = lane_of((ROWS, BLK))
    packed = jnp.zeros((ROWS, BLK), jnp.float32)
    for f in range(FIELDS):
        packed = jnp.where(lanes == f, ref[f, :, lane : lane + 1], packed)
    return packed


def pack_edges(ref, sweep_odd, cross_odd, near_row, far_row, near_col, far_col):
    low, high = ref[:, 0, :], ref[:, ROWS - 1, :]
    near_row[...] = jnp.where(sweep_odd, low, high)
    far_row[...] = jnp.where(sweep_odd, high, low)
    low, high = column(ref, 0), column(ref, COLS - 1)
    near_col[...] = jnp.where(cross_odd, low, high)
    far_col[...] = jnp.where(cross_odd, high, low)


def odd(axis):
    return lax.axis_index(axis) % 2 == 1


def edges_kernel(ref, near_row, far_row, near_col, far_col):
    pack_edges(ref, odd("sweep"), odd("cross"), near_row, far_row, near_col, far_col)


EDGES = (
    jax.ShapeDtypeStruct((FIELDS, COLS), jnp.float32),
    jax.ShapeDtypeStruct((FIELDS, COLS), jnp.float32),
    jax.ShapeDtypeStruct((ROWS, BLK), jnp.float32),
    jax.ShapeDtypeStruct((ROWS, BLK), jnp.float32),
)


def exchange(near_row, far_row, near_col, far_col):
    return (
        swap(near_row, "sweep", 0),
        swap(far_row, "sweep", 1),
        swap(near_col, "cross", 0),
        swap(far_col, "cross", 1),
    )


def neighbours(u, f, sweep_odd, cross_odd, halos):
    near_row, far_row, near_col, far_col = halos
    near, far = near_row[f : f + 1, :], far_row[f : f + 1, :]
    low_row = jnp.where(sweep_odd, near, far)
    high_row = jnp.where(sweep_odd, far, near)
    near, far = near_col[:, f : f + 1], far_col[:, f : f + 1]
    low_col = jnp.where(cross_odd, near, far)
    high_col = jnp.where(cross_odd, far, near)
    rows, lanes = row_of((ROWS, COLS)), lane_of((ROWS, COLS))
    up = jnp.where(rows == 0, low_row, pltpu.roll(u, 1, 0))
    down = jnp.where(rows == ROWS - 1, high_row, pltpu.roll(u, ROWS - 1, 0))
    left = jnp.where(lanes == 0, low_col, pltpu.roll(u, 1, 1))
    right = jnp.where(lanes == COLS - 1, high_col, pltpu.roll(u, COLS - 1, 1))
    return up, down, left, right


def slope(before, centre, after, limited):
    back, front = centre - before, after - centre
    least = jnp.maximum(jnp.minimum(back, front), 0.0) + jnp.minimum(jnp.maximum(back, front), 0.0)
    return jnp.where(limited, least, 0.5 * (back + front))


def split_dot(x, tile):
    tile_high = tile.astype(jnp.bfloat16)
    tile_low = (tile - tile_high.astype(jnp.float32)).astype(jnp.bfloat16)
    x_high = x.astype(jnp.bfloat16).astype(jnp.float32)
    x_low = x - x_high
    left = jnp.concatenate([x_high, x_low], axis=0).astype(jnp.bfloat16)
    right = jnp.concatenate([x_high, jnp.zeros_like(x)], axis=0).astype(jnp.bfloat16)
    moving = jnp.concatenate([left, right], axis=1)
    held = jnp.concatenate([tile_high, tile_low], axis=1)
    out = lax.dot_general(
        moving, held, (((1,), (1,)), ((), ())), preferred_element_type=jnp.float32
    )
    return out[:PAD] + out[PAD:]


def tile_copy(hbm, held, sems, base, c):
    return pltpu.make_async_copy(
        hbm.at[pl.ds(c * CHUNK, CHUNK)], held.at[pl.ds(base + c * CHUNK, CHUNK)], sems.at[base // CHUNK + c]
    )


def remap_kernel(
    source, dest, target, old, offsets, flags, near_row, far_row, near_col, far_col, flux, own,
    send, mass, x, tiles, parts, marks, sems, sent, count,
):
    def start(c, carry):
        tile_copy(flux, tiles, sems, 0, c).start()
        return carry

    def start_own(c, carry):
        tile_copy(own, tiles, sems, TILES, c).start()
        return carry

    lax.fori_loop(0, TILES // CHUNK, start, 0)
    lax.fori_loop(0, BLOCKS // CHUNK, start_own, 0)
    sweep_odd, cross_odd = odd("sweep"), odd("cross")
    halos = (near_row, far_row, near_col, far_col)
    limited = flags[...] > 0
    for f in range(FIELDS):
        u = old[f]
        up, down, left, right = neighbours(u, f, sweep_odd, cross_odd, halos)
        rebuilt = (
            u
            + slope(up, u, down, limited) * offsets[0]
            + slope(left, u, right, limited) * offsets[1]
        )
        x[pl.ds(f, ROWS, stride=2 * PAD), :] = rebuilt[:, :BLK]
        x[pl.ds(PAD + f, ROWS, stride=2 * PAD), :] = rebuilt[:, BLK:]
    for f in range(FIELDS, PAD):
        x[pl.ds(f, BLOCKS, stride=PAD), :] = jnp.full(
            (BLOCKS, BLK), 1.0 if f == FIELDS else 0.0, jnp.float32
        )
    for d in range(SWEEPS):
        count[d] = 0
    marks[...] = jnp.full((SWEEPS, BLK), float(BLOCKS), jnp.float32)
    lanes = lane_of((1, BLK))

    def block(b):
        return x[pl.ds(pl.multiple_of(b * PAD, 8), PAD), :]

    def flux_chunk(c, carry):
        tile_copy(flux, tiles, sems, 0, c).wait()
        first = c * CHUNK
        outs = [split_dot(block(source[first + k]), tiles[first + k]) for k in range(CHUNK)]
        for k in range(CHUNK):
            d = dest[first + k]
            r = count[d]
            count[d] = r + 1
            parts[d, pl.ds(r * WIDE, WIDE), :] = outs[k][:WIDE]
            marks[pl.ds(d, 1), :] = jnp.where(
                lanes == r, target[first + k].astype(jnp.float32), marks[pl.ds(d, 1), :]
            )
        return carry

    lax.fori_loop(0, TILES // CHUNK, flux_chunk, 0)
    for d in range(SWEEPS):
        parts[d, pl.ds(SLOT_ROWS, 8), :] = jnp.broadcast_to(marks[d : d + 1, :], (8, BLK))
    flush = pltpu.make_async_copy(parts, send, sent)
    flush.start()

    def own_chunk(c, carry):
        tile_copy(own, tiles, sems, TILES, c).wait()
        first = c * CHUNK
        for k in range(CHUNK):
            at = pl.ds(pl.multiple_of((first + k) * PAD, 8), PAD)
            mass[at, :] = split_dot(x[at, :], tiles[TILES + first + k])
        return carry

    lax.fori_loop(0, BLOCKS // CHUNK, own_chunk, 0)
    flush.wait()


SUMS = 4


def receive_kernel(
    arrived, mass, density, near_row, far_row, near_col, far_col, parts, marks, found, where, *rest
):
    totals, (part_sems, mark_sem, where_sem) = rest[:SUMS], rest[SUMS:]
    listing = pltpu.make_async_copy(arrived.at[:, pl.ds(SLOT_ROWS, 8), :], marks, mark_sem)
    listing.start()
    copies = [
        pltpu.make_async_copy(arrived.at[s], parts.at[s], part_sems.at[s]) for s in range(SWEEPS)
    ]
    for copy in copies:
        copy.start()
    totals[0][pl.ds(0, BLOCKS * PAD), :] = mass[...]
    for total in totals[1:]:
        total[...] = jnp.zeros(total.shape, jnp.float32)
    listing.wait()
    for s in range(SWEEPS):
        found[s : s + 1, :] = marks[s, 0:1, :].astype(jnp.int32)
    naming = pltpu.make_async_copy(found, where, where_sem)
    naming.start()
    naming.wait()
    for s in range(SWEEPS):
        copies[s].wait()
        for k in range(0, CAP, SUMS):
            at = [pl.ds(pl.multiple_of(where[s, k + j] * PAD, 8), PAD) for j in range(SUMS)]
            old = [totals[j][at[j], :] for j in range(SUMS)]
            for j in range(SUMS):
                totals[j][at[j], :] = old[j] + parts[s, (k + j) * WIDE : (k + j) * WIDE + PAD, :]

    def field(h, f):
        at = pl.ds(h * PAD + f, ROWS, stride=2 * PAD)
        return sum(total[at, :] for total in totals)

    scale = [1.0 / field(h, FIELDS) for h in range(2)]
    for f in range(FIELDS):
        for h in range(2):
            density[f, :, h * BLK : (h + 1) * BLK] = field(h, f) * scale[h]
    pack_edges(density, odd("sweep"), odd("cross"), near_row, far_row, near_col, far_col)


def smooth_kernel(density, near_row, far_row, near_col, far_col, out):
    halos = (near_row, far_row, near_col, far_col)
    for f in range(FIELDS):
        u = density[f]
        up, down, left, right = neighbours(u, f, odd("sweep"), odd("cross"), halos)
        out[f] = u + SMOOTHING * (up + down + left + right - 4.0 * u)


def params(mib):
    return pltpu.CompilerParams(vmem_limit_bytes=mib * 1024 * 1024)


def body(
    old_state, offsets, limiter_flags, self_tiles, flux_tiles, tile_source, tile_dest, tile_target
):
    vm, sm, hbm = (pl.BlockSpec(memory_space=m) for m in (VMEM, SMEM, pl.ANY))
    dma = pltpu.SemaphoreType.DMA
    edges = pl.pallas_call(
        edges_kernel, out_shape=EDGES, in_specs=[vm], out_specs=(vm,) * 4,
        compiler_params=params(16), name="edges",
    )(old_state)
    halos = exchange(*edges)
    send, mass = pl.pallas_call(
        remap_kernel,
        out_shape=(
            jax.ShapeDtypeStruct((SWEEPS, PART_ROWS, BLK), jnp.float32),
            jax.ShapeDtypeStruct((BLOCKS * PAD, BLK), jnp.float32),
        ),
        in_specs=[sm] * 3 + [vm] * 7 + [hbm] * 2,
        out_specs=(hbm, vm),
        scratch_shapes=[
            VMEM((BLOCKS * PAD, BLK), jnp.float32),
            VMEM((TILES + BLOCKS, BLK, BLK), jnp.float32),
            VMEM((SWEEPS, PART_ROWS, BLK), jnp.float32),
            VMEM((SWEEPS, BLK), jnp.float32),
            dma(((TILES + BLOCKS) // CHUNK,)),
            dma,
            SMEM((SWEEPS,), jnp.int32),
        ],
        compiler_params=params(48),
        cost_estimate=pl.CostEstimate(
            flops=2 * 6 * (TILES + BLOCKS) * PAD * BLK * BLK,
            bytes_accessed=(TILES + BLOCKS) * BLK * BLK * 4,
            transcendentals=0,
        ),
        name="remap",
    )(
        tile_source, tile_dest.reshape(TILES), tile_target, old_state, offsets, limiter_flags,
        *halos, flux_tiles, self_tiles,
    )
    arrived = lax.all_to_all(send, "sweep", split_axis=0, concat_axis=0, tiled=True)
    density, *edges = pl.pallas_call(
        receive_kernel,
        out_shape=(jax.ShapeDtypeStruct((FIELDS, ROWS, COLS), jnp.float32),) + EDGES,
        in_specs=[hbm, vm],
        out_specs=(vm,) * 5,
        scratch_shapes=[
            VMEM((SWEEPS, PART_ROWS, BLK), jnp.float32),
            VMEM((SWEEPS, 8, BLK), jnp.float32),
            VMEM((SWEEPS, BLK), jnp.int32),
            SMEM((SWEEPS, BLK), jnp.int32),
        ]
        + [VMEM(((BLOCKS + 1) * PAD, BLK), jnp.float32)] * SUMS
        + [dma((SWEEPS,)), dma, dma],
        compiler_params=params(32),
        name="receive",
    )(arrived, mass)
    halos = exchange(*edges)
    return pl.pallas_call(
        smooth_kernel,
        out_shape=jax.ShapeDtypeStruct((FIELDS, ROWS, COLS), jnp.float32),
        in_specs=[vm] * 5,
        out_specs=vm,
        compiler_params=params(16),
        name="smooth",
    )(density, *halos)


def solution(mesh):
    placed = (
        P(None, "sweep", "cross"),
        P(None, "sweep", "cross"),
        P("sweep", "cross"),
        P(("sweep", "cross"), None, None),
        P(("sweep", "cross"), None, None),
        P(("sweep", "cross")),
        P(("sweep", "cross"), None),
        P(("sweep", "cross")),
    )
    return jax.shard_map(
        body, mesh=mesh, in_specs=placed, out_specs=P(None, "sweep", "cross"), check_vma=False
    )
```

```python
import functools

import jax
import jax.numpy as jnp
from jax import lax
from jax.experimental import pallas as pl
from jax.experimental.pallas import tpu as pltpu
from jax.sharding import PartitionSpec as P

SMOOTHING = 0.1
FIELDS, ROWS, COLS = 20, 48, 256
BLOCKS, BLK = 96, 128
TILES, CAP = 192, 24
SWEEPS, CROSSES = 16, 8
PAD = 24
WIDE = FIELDS + 1
SLOT_ROWS = CAP * WIDE
PART_ROWS = SLOT_ROWS + 8
CHUNK = 24
VMEM = pltpu.VMEM
SMEM = pltpu.SMEM


def pairs(count, shift):
    return [(i, (((i + shift) ^ 1) - shift) % count) for i in range(count)]


def swap(values, axis, shift):
    return lax.ppermute(values, axis, pairs(lax.axis_size(axis), shift))


def lane_of(shape):
    return lax.broadcasted_iota(jnp.int32, shape, len(shape) - 1)


def row_of(shape):
    return lax.broadcasted_iota(jnp.int32, shape, len(shape) - 2)


def column(ref, lane):
    lanes = lane_of((ROWS, BLK))
    packed = jnp.zeros((ROWS, BLK), jnp.float32)
    for f in range(FIELDS):
        packed = jnp.where(lanes == f, ref[f, :, lane : lane + 1], packed)
    return packed


def pack_edges(ref, sweep_odd, cross_odd, near_row, far_row, near_col, far_col):
    low, high = ref[:, 0, :], ref[:, ROWS - 1, :]
    near_row[...] = jnp.where(sweep_odd, low, high)
    far_row[...] = jnp.where(sweep_odd, high, low)
    low, high = column(ref, 0), column(ref, COLS - 1)
    near_col[...] = jnp.where(cross_odd, low, high)
    far_col[...] = jnp.where(cross_odd, high, low)


def edges_kernel(ref, near_row, far_row, near_col, far_col):
    pack_edges(ref, odd("sweep"), odd("cross"), near_row, far_row, near_col, far_col)


EDGES = (
    jax.ShapeDtypeStruct((FIELDS, COLS), jnp.float32),
    jax.ShapeDtypeStruct((FIELDS, COLS), jnp.float32),
    jax.ShapeDtypeStruct((ROWS, BLK), jnp.float32),
    jax.ShapeDtypeStruct((ROWS, BLK), jnp.float32),
)


def exchange(near_row, far_row, near_col, far_col):
    return (
        swap(near_row, "sweep", 0),
        swap(far_row, "sweep", 1),
        swap(near_col, "cross", 0),
        swap(far_col, "cross", 1),
    )


def odd(axis):
    return lax.axis_index(axis) % 2 == 1


def sides(axis, near, far):
    at, last = lax.axis_index(axis), lax.axis_size(axis) - 1
    before = jnp.where(at == 0, 0.0, jnp.where(odd(axis), near, far))
    after = jnp.where(at == last, 0.0, jnp.where(odd(axis), far, near))
    return before, after


def neighbours(u, f, rows, cols):
    low_row, high_row = (side[f : f + 1, :] for side in rows)
    low_col, high_col = (side[:, f : f + 1] for side in cols)
    at_row, at_lane = row_of((ROWS, COLS)), lane_of((ROWS, COLS))
    up = jnp.where(at_row == 0, low_row, pltpu.roll(u, 1, 0))
    down = jnp.where(at_row == ROWS - 1, high_row, pltpu.roll(u, ROWS - 1, 0))
    left = jnp.where(at_lane == 0, low_col, pltpu.roll(u, 1, 1))
    right = jnp.where(at_lane == COLS - 1, high_col, pltpu.roll(u, COLS - 1, 1))
    return up, down, left, right


def slope(before, centre, after, limited):
    back, front = centre - before, after - centre
    least = jnp.maximum(jnp.minimum(back, front), 0.0) + jnp.minimum(jnp.maximum(back, front), 0.0)
    return jnp.where(limited, least, 0.5 * (back + front))


def split_dot(x, tile):
    tile_high = tile.astype(jnp.bfloat16)
    tile_low = (tile - tile_high.astype(jnp.float32)).astype(jnp.bfloat16)
    x_high = x.astype(jnp.bfloat16).astype(jnp.float32)
    x_low = x - x_high
    left = jnp.concatenate([x_high, x_low], axis=0).astype(jnp.bfloat16)
    right = jnp.concatenate([x_high, jnp.zeros_like(x)], axis=0).astype(jnp.bfloat16)
    moving = jnp.concatenate([left, right], axis=1)
    held = jnp.concatenate([tile_high, tile_low], axis=1)
    out = lax.dot_general(
        moving, held, (((1,), (1,)), ((), ())), preferred_element_type=jnp.float32
    )
    return out[:PAD] + out[PAD:]


def tile_copy(hbm, held, sems, base, c):
    return pltpu.make_async_copy(
        hbm.at[pl.ds(c * CHUNK, CHUNK)], held.at[pl.ds(base + c * CHUNK, CHUNK)], sems.at[base // CHUNK + c]
    )


def remap_kernel(
    source_in, dest_in, target_in, old_in, offsets_in, flags_in, near_row, far_row, near_col, far_col,
    flux, own, parts, mass, source, dest, target, old, offsets, flags, x, tiles, marks,
    sems, count, input_sems,
):
    inputs = [
        pltpu.make_async_copy(held, here, input_sems.at[i])
        for i, (held, here) in enumerate(
            (
                (old_in, old), (offsets_in, offsets), (flags_in, flags),
                (source_in, source), (dest_in, dest), (target_in, target),
            )
        )
    ]
    for copy in inputs:
        copy.start()

    def start(c, carry):
        tile_copy(flux, tiles, sems, 0, c).start()
        return carry

    def start_own(c, carry):
        tile_copy(own, tiles, sems, TILES, c).start()
        return carry

    lax.fori_loop(0, TILES // CHUNK, start, 0)
    lax.fori_loop(0, BLOCKS // CHUNK, start_own, 0)
    rows = sides("sweep", near_row[...], far_row[...])
    cols = sides("cross", near_col[...], far_col[...])
    for copy in inputs:
        copy.wait()
    limited = flags[...] > 0
    for f in range(FIELDS):
        u = old[f]
        up, down, left, right = neighbours(u, f, rows, cols)
        rebuilt = (
            u
            + slope(up, u, down, limited) * offsets[0]
            + slope(left, u, right, limited) * offsets[1]
        )
        x[pl.ds(f, ROWS, stride=2 * PAD), :] = rebuilt[:, :BLK]
        x[pl.ds(PAD + f, ROWS, stride=2 * PAD), :] = rebuilt[:, BLK:]
    for f in range(FIELDS, PAD):
        x[pl.ds(f, BLOCKS, stride=PAD), :] = jnp.full(
            (BLOCKS, BLK), 1.0 if f == FIELDS else 0.0, jnp.float32
        )
    for d in range(SWEEPS):
        count[d] = 0
    marks[...] = jnp.full((SWEEPS, BLK), float(BLOCKS), jnp.float32)
    lanes = lane_of((1, BLK))

    def block(b):
        return x[pl.ds(pl.multiple_of(b * PAD, 8), PAD), :]

    def flux_chunk(c, carry):
        tile_copy(flux, tiles, sems, 0, c).wait()
        first = c * CHUNK
        outs = [split_dot(block(source[first + k]), tiles[first + k]) for k in range(CHUNK)]
        for k in range(CHUNK):
            d = dest[first + k]
            r = count[d]
            count[d] = r + 1
            parts[d, pl.ds(r * WIDE, WIDE), :] = outs[k][:WIDE]
            marks[pl.ds(d, 1), :] = jnp.where(
                lanes == r, target[first + k].astype(jnp.float32), marks[pl.ds(d, 1), :]
            )
        return carry

    lax.fori_loop(0, TILES // CHUNK, flux_chunk, 0)
    for d in range(SWEEPS):
        parts[d, pl.ds(SLOT_ROWS, 8), :] = jnp.broadcast_to(marks[d : d + 1, :], (8, BLK))

    def own_chunk(c, carry):
        tile_copy(own, tiles, sems, TILES, c).wait()
        first = c * CHUNK
        for k in range(CHUNK):
            at = pl.ds(pl.multiple_of((first + k) * PAD, 8), PAD)
            mass[at, :] = split_dot(x[at, :], tiles[TILES + first + k])
        return carry

    lax.fori_loop(0, BLOCKS // CHUNK, own_chunk, 0)


SUMS = 4


def receive_kernel(
    parts, mass, density, near_row, far_row, near_col, far_col, found, where, sem, *totals
):
    for s in range(SWEEPS):
        found[s : s + 1, :] = parts[s, SLOT_ROWS : SLOT_ROWS + 1, :].astype(jnp.int32)
    naming = pltpu.make_async_copy(found, where, sem)
    naming.start()
    totals[0][pl.ds(0, BLOCKS * PAD), :] = mass[...]
    for total in totals[1:]:
        total[...] = jnp.zeros(total.shape, jnp.float32)
    naming.wait()
    for s in range(SWEEPS):
        for k in range(0, CAP, SUMS):
            at = [pl.ds(pl.multiple_of(where[s, k + j] * PAD, 8), PAD) for j in range(SUMS)]
            old = [totals[j][at[j], :] for j in range(SUMS)]
            for j in range(SUMS):
                totals[j][at[j], :] = old[j] + parts[s, (k + j) * WIDE : (k + j) * WIDE + PAD, :]

    def field(h, f):
        at = pl.ds(h * PAD + f, ROWS, stride=2 * PAD)
        return sum(total[at, :] for total in totals)

    scale = [1.0 / field(h, FIELDS) for h in range(2)]
    for f in range(FIELDS):
        for h in range(2):
            density[f, :, h * BLK : (h + 1) * BLK] = field(h, f) * scale[h]
    pack_edges(density, odd("sweep"), odd("cross"), near_row, far_row, near_col, far_col)


def smooth_kernel(density, near_row, far_row, near_col, far_col, out):
    rows = sides("sweep", near_row[...], far_row[...])
    cols = sides("cross", near_col[...], far_col[...])
    for f in range(FIELDS):
        u = density[f]
        up, down, left, right = neighbours(u, f, rows, cols)
        out[f] = u + SMOOTHING * (up + down + left + right - 4.0 * u)


def in_place(held):
    return pltpu.with_memory_space_constraint(held, pltpu.HBM)


def params(mib):
    return pltpu.CompilerParams(vmem_limit_bytes=mib * 1024 * 1024)


def body(
    old_state, offsets, limiter_flags, self_tiles, flux_tiles, tile_source, tile_dest, tile_target
):
    vm, hbm = (pl.BlockSpec(memory_space=m) for m in (VMEM, pltpu.HBM))
    dma = pltpu.SemaphoreType.DMA
    edges = pl.pallas_call(
        edges_kernel, out_shape=EDGES, in_specs=[vm], out_specs=(vm,) * 4,
        compiler_params=params(16), name="edges",
    )(old_state)
    halos = exchange(*edges)
    send, mass = pl.pallas_call(
        remap_kernel,
        out_shape=(
            jax.ShapeDtypeStruct((SWEEPS, PART_ROWS, BLK), jnp.float32),
            jax.ShapeDtypeStruct((BLOCKS * PAD, BLK), jnp.float32),
        ),
        in_specs=[hbm] * 6 + [vm] * 4 + [hbm] * 2,
        out_specs=(vm, vm),
        scratch_shapes=[SMEM((TILES,), jnp.int32)] * 3
        + [
            VMEM((FIELDS, ROWS, COLS), jnp.float32),
            VMEM((2, ROWS, COLS), jnp.float32),
            VMEM((ROWS, COLS), jnp.int32),
            VMEM((BLOCKS * PAD, BLK), jnp.float32),
            VMEM((TILES + BLOCKS, BLK, BLK), jnp.float32),
            VMEM((SWEEPS, BLK), jnp.float32),
            dma(((TILES + BLOCKS) // CHUNK,)),
            SMEM((SWEEPS,), jnp.int32),
            dma((6,)),
        ],
        compiler_params=params(48),
        cost_estimate=pl.CostEstimate(
            flops=2 * 6 * (TILES + BLOCKS) * PAD * BLK * BLK,
            bytes_accessed=(TILES + BLOCKS) * BLK * BLK * 4,
            transcendentals=0,
        ),
        name="remap",
    )(
        *(
            in_place(held)
            for held in (
                tile_source, tile_dest.reshape(TILES), tile_target, old_state, offsets, limiter_flags
            )
        ),
        *halos,
        in_place(flux_tiles),
        in_place(self_tiles),
    )
    arrived = lax.all_to_all(send, "sweep", split_axis=0, concat_axis=0, tiled=True)
    density, *edges = pl.pallas_call(
        receive_kernel,
        out_shape=(jax.ShapeDtypeStruct((FIELDS, ROWS, COLS), jnp.float32),) + EDGES,
        in_specs=[vm, vm],
        out_specs=(vm,) * 5,
        scratch_shapes=[VMEM((SWEEPS, BLK), jnp.int32), SMEM((SWEEPS, BLK), jnp.int32), dma]
        + [VMEM(((BLOCKS + 1) * PAD, BLK), jnp.float32)] * SUMS,
        compiler_params=params(32),
        name="receive",
    )(arrived, mass)
    halos = exchange(*edges)
    return pl.pallas_call(
        smooth_kernel,
        out_shape=jax.ShapeDtypeStruct((FIELDS, ROWS, COLS), jnp.float32),
        in_specs=[vm] * 5,
        out_specs=vm,
        compiler_params=params(16),
        name="smooth",
    )(density, *halos)


def solution(mesh):
    placed = (
        P(None, "sweep", "cross"),
        P(None, "sweep", "cross"),
        P("sweep", "cross"),
        P(("sweep", "cross"), None, None),
        P(("sweep", "cross"), None, None),
        P(("sweep", "cross")),
        P(("sweep", "cross"), None),
        P(("sweep", "cross")),
    )
    return jax.shard_map(
        body, mesh=mesh, in_specs=placed, out_specs=P(None, "sweep", "cross"), check_vma=False
    )
```

```python
import functools

import jax
import jax.numpy as jnp
from jax import lax
from jax.experimental import pallas as pl
from jax.experimental.pallas import tpu as pltpu
from jax.sharding import PartitionSpec as P

SMOOTHING = 0.1
FIELDS, ROWS, COLS = 20, 48, 256
BLOCKS, BLK = 96, 128
TILES, CAP = 192, 24
SWEEPS, CROSSES = 16, 8
PAD = 24
WIDE = FIELDS + 1
SLOT_ROWS = CAP * WIDE
PART_ROWS = SLOT_ROWS + 8
CHUNK = 48
VMEM = pltpu.VMEM
SMEM = pltpu.SMEM


def pairs(count, shift):
    return [(i, (((i + shift) ^ 1) - shift) % count) for i in range(count)]


def swap(values, axis, shift):
    return lax.ppermute(values, axis, pairs(lax.axis_size(axis), shift))


def lane_of(shape):
    return lax.broadcasted_iota(jnp.int32, shape, len(shape) - 1)


def row_of(shape):
    return lax.broadcasted_iota(jnp.int32, shape, len(shape) - 2)


def column(ref, lane):
    lanes = lane_of((ROWS, BLK))
    packed = jnp.zeros((ROWS, BLK), jnp.float32)
    for f in range(FIELDS):
        packed = jnp.where(lanes == f, ref[f, :, lane : lane + 1], packed)
    return packed


def pack_edges(ref, sweep_odd, cross_odd, near_row, far_row, near_col, far_col):
    low, high = ref[:, 0, :], ref[:, ROWS - 1, :]
    near_row[...] = jnp.where(sweep_odd, low, high)
    far_row[...] = jnp.where(sweep_odd, high, low)
    low, high = column(ref, 0), column(ref, COLS - 1)
    near_col[...] = jnp.where(cross_odd, low, high)
    far_col[...] = jnp.where(cross_odd, high, low)


def edges_kernel(ref, near_row, far_row, near_col, far_col, held):
    pack_edges(ref, odd("sweep"), odd("cross"), near_row, far_row, near_col, far_col)


EDGES = (
    jax.ShapeDtypeStruct((FIELDS, COLS), jnp.float32),
    jax.ShapeDtypeStruct((FIELDS, COLS), jnp.float32),
    jax.ShapeDtypeStruct((ROWS, BLK), jnp.float32),
    jax.ShapeDtypeStruct((ROWS, BLK), jnp.float32),
)


def exchange(near_row, far_row, near_col, far_col):
    return (
        swap(near_row, "sweep", 0),
        swap(far_row, "sweep", 1),
        swap(near_col, "cross", 0),
        swap(far_col, "cross", 1),
    )


def odd(axis):
    return lax.axis_index(axis) % 2 == 1


def sides(axis, near, far):
    at, last = lax.axis_index(axis), lax.axis_size(axis) - 1
    before = jnp.where(at == 0, 0.0, jnp.where(odd(axis), near, far))
    after = jnp.where(at == last, 0.0, jnp.where(odd(axis), far, near))
    return before, after


def neighbours(u, f, rows, cols):
    low_row, high_row = (side[f : f + 1, :] for side in rows)
    low_col, high_col = (side[:, f : f + 1] for side in cols)
    at_row, at_lane = row_of((ROWS, COLS)), lane_of((ROWS, COLS))
    up = jnp.where(at_row == 0, low_row, pltpu.roll(u, 1, 0))
    down = jnp.where(at_row == ROWS - 1, high_row, pltpu.roll(u, ROWS - 1, 0))
    left = jnp.where(at_lane == 0, low_col, pltpu.roll(u, 1, 1))
    right = jnp.where(at_lane == COLS - 1, high_col, pltpu.roll(u, COLS - 1, 1))
    return up, down, left, right


def span(back, front, limited):
    least = jnp.maximum(jnp.minimum(back, front), 0.0) + jnp.minimum(jnp.maximum(back, front), 0.0)
    return jnp.where(limited, least, 0.5 * (back + front))


def split_dot(x, tile):
    tile_high = tile.astype(jnp.bfloat16)
    tile_low = (tile - tile_high.astype(jnp.float32)).astype(jnp.bfloat16)
    x_high = x.astype(jnp.bfloat16).astype(jnp.float32)
    x_low = x - x_high
    left = jnp.concatenate([x_high, x_low], axis=0).astype(jnp.bfloat16)
    right = jnp.concatenate([x_high, jnp.zeros_like(x)], axis=0).astype(jnp.bfloat16)
    moving = jnp.concatenate([left, right], axis=1)
    held = jnp.concatenate([tile_high, tile_low], axis=1)
    out = lax.dot_general(
        moving, held, (((1,), (1,)), ((), ())), preferred_element_type=jnp.float32
    )
    return out[:PAD] + out[PAD:]


def stage_kernel(old, offsets_in, flags_in, own_in, x, own, cols, rows, offsets, flags, sems):
    copies = [
        pltpu.make_async_copy(held, here, sems.at[i])
        for i, (held, here) in enumerate(((offsets_in, offsets), (flags_in, flags), (own_in, own)))
    ]
    for copy in copies:
        copy.start()
    for f in range(FIELDS, PAD):
        x[pl.ds(f, BLOCKS, stride=PAD), :] = jnp.full(
            (BLOCKS, BLK), 1.0 if f == FIELDS else 0.0, jnp.float32
        )
    for copy in copies[:2]:
        copy.wait()
    limited = flags[...] > 0
    none = jnp.zeros((FIELDS, COLS), jnp.float32)
    none_col = jnp.zeros((ROWS, BLK), jnp.float32)
    for f in range(FIELDS):
        u = old[f]
        up, down, left, right = neighbours(u, f, (none, none), (none_col, none_col))
        rebuilt = (
            u
            + span(u - up, down - u, limited) * offsets[0]
            + span(u - left, right - u, limited) * offsets[1]
        )
        x[pl.ds(f, ROWS, stride=2 * PAD), :] = rebuilt[:, :BLK]
        x[pl.ds(PAD + f, ROWS, stride=2 * PAD), :] = rebuilt[:, BLK:]
    for side, (edge, beside) in enumerate(((0, 1), (COLS - 1, COLS - 2))):
        value, next_value = column(old, edge), column(old, beside)
        near, sign = value - next_value, (1.0, -1.0)[side]
        flag = flags[:, edge : edge + 1] > 0
        cols[side, 0] = value
        cols[side, 1] = -sign * near
        cols[side, 2] = span(sign * value, -sign * near, flag)
        cols[side, 3] = jnp.broadcast_to(offsets[1, :, edge : edge + 1], (ROWS, BLK))
        cols[side, 4] = jnp.broadcast_to(flags[:, edge : edge + 1], (ROWS, BLK)).astype(jnp.float32)
    for side, (edge, beside) in enumerate(((0, 1), (ROWS - 1, ROWS - 2))):
        value, next_value = old[:, edge, :], old[:, beside, :]
        near, sign = value - next_value, (1.0, -1.0)[side]
        flag = flags[edge : edge + 1, :] > 0
        rows[side, 0] = value
        rows[side, 1] = -sign * near
        rows[side, 2] = span(sign * value, -sign * near, flag)
        rows[side, 3] = jnp.broadcast_to(offsets[0, edge : edge + 1, :], (FIELDS, COLS))
        rows[side, 4] = jnp.broadcast_to(flags[edge : edge + 1, :], (FIELDS, COLS)).astype(jnp.float32)
    copies[2].wait()


def edge_change(ref, side, beyond):
    outer = ref[side, 0] - beyond if side == 0 else beyond - ref[side, 0]
    return (span(outer, ref[side, 1], ref[side, 4] > 0) - ref[side, 2]) * ref[side, 3]


def remap_kernel(
    source_in, dest_in, target_in, near_row, far_row, near_col, far_col, start_x, cols, rows, own,
    flux, parts, mass, source, dest, target, x, tiles, marks, sems, count, input_sems,
):
    inputs = [
        pltpu.make_async_copy(held, here, input_sems.at[i])
        for i, (held, here) in enumerate(((source_in, source), (dest_in, dest), (target_in, target)))
    ]
    for copy in inputs:
        copy.start()

    def tile_copy(c):
        span_of = pl.ds(c * CHUNK, CHUNK)
        return pltpu.make_async_copy(flux.at[span_of], tiles.at[span_of], sems.at[c])

    for c in range(TILES // CHUNK):
        tile_copy(c).start()
    x[...] = start_x[...]
    for side, beyond in enumerate(sides("sweep", near_row[...], far_row[...])):
        change = edge_change(rows, side, beyond)
        for h in range(2):
            at = pl.ds(((ROWS - 1) * side * 2 + h) * PAD, FIELDS)
            x[at, :] += change[:, h * BLK : (h + 1) * BLK]
    lanes = lane_of((ROWS, BLK))
    for side, beyond in enumerate(sides("cross", near_col[...], far_col[...])):
        change = edge_change(cols, side, beyond)
        for f in range(FIELDS):
            at = pl.ds(side * PAD + f, ROWS, stride=2 * PAD)
            x[at, :] += jnp.where(lanes == (BLK - 1) * side, change[:, f : f + 1], 0.0)
    marks[...] = jnp.full((SWEEPS, BLK), float(BLOCKS), jnp.float32)
    lanes = lane_of((1, BLK))

    def block(b):
        return x[pl.ds(pl.multiple_of(b * PAD, 8), PAD), :]

    def own_chunk(c, carry):
        first = c * CHUNK
        outs = [split_dot(block(first + k), own[first + k]) for k in range(CHUNK)]
        for k in range(CHUNK):
            mass[pl.ds(pl.multiple_of((first + k) * PAD, 8), PAD), :] = outs[k]
        return carry

    lax.fori_loop(0, BLOCKS // CHUNK, own_chunk, 0)
    for copy in inputs:
        copy.wait()
    for d in range(SWEEPS):
        count[d] = 0

    def flux_chunk(c, carry):
        tile_copy(c).wait()
        first = c * CHUNK
        outs = [split_dot(block(source[first + k]), tiles[first + k]) for k in range(CHUNK)]
        for k in range(CHUNK):
            d = dest[first + k]
            r = count[d]
            count[d] = r + 1
            parts[d, pl.ds(r * WIDE, WIDE), :] = outs[k][:WIDE]
            marks[pl.ds(d, 1), :] = jnp.where(
                lanes == r, target[first + k].astype(jnp.float32), marks[pl.ds(d, 1), :]
            )
        return carry

    lax.fori_loop(0, TILES // CHUNK, flux_chunk, 0)
    for d in range(SWEEPS):
        parts[d, pl.ds(SLOT_ROWS, 8), :] = jnp.broadcast_to(marks[d : d + 1, :], (8, BLK))


SUMS = 4


def receive_kernel(
    parts, mass, density, near_row, far_row, near_col, far_col, found, where, sem, *totals
):
    for s in range(SWEEPS):
        found[s : s + 1, :] = parts[s, SLOT_ROWS : SLOT_ROWS + 1, :].astype(jnp.int32)
    naming = pltpu.make_async_copy(found, where, sem)
    naming.start()
    totals[0][pl.ds(0, BLOCKS * PAD), :] = mass[...]
    for total in totals[1:]:
        total[...] = jnp.zeros(total.shape, jnp.float32)
    naming.wait()
    for s in range(SWEEPS):
        for k in range(0, CAP, SUMS):
            at = [pl.ds(pl.multiple_of(where[s, k + j] * PAD, 8), PAD) for j in range(SUMS)]
            old = [totals[j][at[j], :] for j in range(SUMS)]
            for j in range(SUMS):
                totals[j][at[j], :] = old[j] + parts[s, (k + j) * WIDE : (k + j) * WIDE + PAD, :]

    def field(h, f):
        at = pl.ds(h * PAD + f, ROWS, stride=2 * PAD)
        return sum(total[at, :] for total in totals)

    scale = [1.0 / field(h, FIELDS) for h in range(2)]
    for f in range(FIELDS):
        for h in range(2):
            density[f, :, h * BLK : (h + 1) * BLK] = field(h, f) * scale[h]
    pack_edges(density, odd("sweep"), odd("cross"), near_row, far_row, near_col, far_col)


def smooth_kernel(density, near_row, far_row, near_col, far_col, out):
    rows = sides("sweep", near_row[...], far_row[...])
    cols = sides("cross", near_col[...], far_col[...])
    for f in range(FIELDS):
        u = density[f]
        up, down, left, right = neighbours(u, f, rows, cols)
        out[f] = u + SMOOTHING * (up + down + left + right - 4.0 * u)


def in_place(held):
    return pltpu.with_memory_space_constraint(held, pltpu.HBM)


def params(mib):
    return pltpu.CompilerParams(vmem_limit_bytes=mib * 1024 * 1024)


def body(
    old_state, offsets, limiter_flags, self_tiles, flux_tiles, tile_source, tile_dest, tile_target
):
    vm, hbm = (pl.BlockSpec(memory_space=m) for m in (VMEM, pltpu.HBM))
    dma = pltpu.SemaphoreType.DMA
    shape = lambda *sizes: jax.ShapeDtypeStruct(sizes, jnp.float32)
    *edges, held = pl.pallas_call(
        edges_kernel, out_shape=EDGES + (shape(FIELDS, ROWS, COLS),), in_specs=[vm], out_specs=(vm,) * 5,
        input_output_aliases={0: 4}, compiler_params=params(16), name="edges",
    )(old_state)
    halos = exchange(*edges)
    start_x, own, cols, rows = pl.pallas_call(
        stage_kernel,
        out_shape=(
            shape(BLOCKS * PAD, BLK), shape(BLOCKS, BLK, BLK),
            shape(2, 5, ROWS, BLK), shape(2, 5, FIELDS, COLS),
        ),
        in_specs=[vm] + [hbm] * 3,
        out_specs=(vm,) * 4,
        scratch_shapes=[VMEM((2, ROWS, COLS), jnp.float32), VMEM((ROWS, COLS), jnp.int32), dma((3,))],
        compiler_params=params(16),
        cost_estimate=pl.CostEstimate(
            flops=40 * FIELDS * ROWS * COLS, bytes_accessed=BLOCKS * BLK * BLK * 4, transcendentals=0
        ),
        name="stage",
    )(held, in_place(offsets), in_place(limiter_flags), in_place(self_tiles))
    send, mass = pl.pallas_call(
        remap_kernel,
        out_shape=(shape(SWEEPS, PART_ROWS, BLK), shape(BLOCKS * PAD, BLK)),
        in_specs=[hbm] * 3 + [vm] * 8 + [hbm],
        out_specs=(vm, vm),
        scratch_shapes=[SMEM((TILES,), jnp.int32)] * 3
        + [
            VMEM((BLOCKS * PAD, BLK), jnp.float32),
            VMEM((TILES, BLK, BLK), jnp.float32),
            VMEM((SWEEPS, BLK), jnp.float32),
            dma((TILES // CHUNK,)),
            SMEM((SWEEPS,), jnp.int32),
            dma((3,)),
        ],
        compiler_params=params(32),
        cost_estimate=pl.CostEstimate(
            flops=2 * 6 * (TILES + BLOCKS) * PAD * BLK * BLK,
            bytes_accessed=TILES * BLK * BLK * 4,
            transcendentals=0,
        ),
        name="remap",
    )(
        *(in_place(held) for held in (tile_source, tile_dest.reshape(TILES), tile_target)),
        *halos, start_x, cols, rows, own, in_place(flux_tiles),
    )
    arrived = lax.all_to_all(send, "sweep", split_axis=0, concat_axis=0, tiled=True)
    density, *edges = pl.pallas_call(
        receive_kernel,
        out_shape=(jax.ShapeDtypeStruct((FIELDS, ROWS, COLS), jnp.float32),) + EDGES,
        in_specs=[vm, vm],
        out_specs=(vm,) * 5,
        scratch_shapes=[VMEM((SWEEPS, BLK), jnp.int32), SMEM((SWEEPS, BLK), jnp.int32), dma]
        + [VMEM(((BLOCKS + 1) * PAD, BLK), jnp.float32)] * SUMS,
        compiler_params=params(32),
        name="receive",
    )(arrived, mass)
    halos = exchange(*edges)
    return pl.pallas_call(
        smooth_kernel,
        out_shape=jax.ShapeDtypeStruct((FIELDS, ROWS, COLS), jnp.float32),
        in_specs=[vm] * 5,
        out_specs=vm,
        compiler_params=params(16),
        name="smooth",
    )(density, *halos)


def solution(mesh):
    placed = (
        P(None, "sweep", "cross"),
        P(None, "sweep", "cross"),
        P("sweep", "cross"),
        P(("sweep", "cross"), None, None),
        P(("sweep", "cross"), None, None),
        P(("sweep", "cross")),
        P(("sweep", "cross"), None),
        P(("sweep", "cross")),
    )
    return jax.shard_map(
        body, mesh=mesh, in_specs=placed, out_specs=P(None, "sweep", "cross"), check_vma=False
    )
```

```python
import functools

import jax
import jax.numpy as jnp
from jax import lax
from jax.experimental import pallas as pl
from jax.experimental.pallas import tpu as pltpu
from jax.sharding import PartitionSpec as P

SMOOTHING = 0.1
FIELDS, ROWS, COLS = 20, 48, 256
BLOCKS, BLK = 96, 128
TILES, CAP = 192, 24
SWEEPS, CROSSES = 16, 8
PAD = 24
EDGE_ROWS = 32
WIDE = FIELDS + 1
SLOT_ROWS = CAP * WIDE
PART_ROWS = SLOT_ROWS + 8
CHUNK = 48
VMEM = pltpu.VMEM
SMEM = pltpu.SMEM


def pairs(count, shift):
    return [(i, (((i + shift) ^ 1) - shift) % count) for i in range(count)]


def swap(values, axis, shift):
    return lax.ppermute(values, axis, pairs(lax.axis_size(axis), shift))


def lane_of(shape):
    return lax.broadcasted_iota(jnp.int32, shape, len(shape) - 1)


def row_of(shape):
    return lax.broadcasted_iota(jnp.int32, shape, len(shape) - 2)


def column(ref, lane):
    lanes = lane_of((ROWS, BLK))
    packed = jnp.zeros((ROWS, BLK), jnp.float32)
    for f in range(FIELDS):
        packed = jnp.where(lanes == f, ref[f, :, lane : lane + 1], packed)
    return packed


def pack_edges(ref, sweep_odd, cross_odd, far_row, near_row, far_col, near_col):
    low, high = ref[:, 0, :], ref[:, ROWS - 1, :]
    near_row[:FIELDS, :] = jnp.where(sweep_odd, low, high)
    far_row[:FIELDS, :] = jnp.where(sweep_odd, high, low)
    low, high = column(ref, 0), column(ref, COLS - 1)
    near_col[...] = jnp.where(cross_odd, low, high)
    far_col[...] = jnp.where(cross_odd, high, low)


def edges_kernel(ref, far_row, near_row, far_col, near_col, held):
    pack_edges(ref, odd("sweep"), odd("cross"), far_row, near_row, far_col, near_col)


EDGES = (
    jax.ShapeDtypeStruct((EDGE_ROWS, COLS), jnp.float32),
    jax.ShapeDtypeStruct((EDGE_ROWS, COLS), jnp.float32),
    jax.ShapeDtypeStruct((ROWS, BLK), jnp.float32),
    jax.ShapeDtypeStruct((ROWS, BLK), jnp.float32),
)


def exchange(far_row, near_row, far_col, near_col):
    return (
        swap(far_row, "sweep", 1),
        swap(near_row, "sweep", 0),
        swap(far_col, "cross", 1),
        swap(near_col, "cross", 0),
    )


def odd(axis):
    return lax.axis_index(axis) % 2 == 1


def sides(axis, near, far):
    at, last = lax.axis_index(axis), lax.axis_size(axis) - 1
    before = jnp.where(at == 0, 0.0, jnp.where(odd(axis), near, far))
    after = jnp.where(at == last, 0.0, jnp.where(odd(axis), far, near))
    return before, after


def neighbours(u, f, rows, cols):
    low_row, high_row = (side[f : f + 1, :] for side in rows)
    low_col, high_col = (side[:, f : f + 1] for side in cols)
    at_row, at_lane = row_of((ROWS, COLS)), lane_of((ROWS, COLS))
    up = jnp.where(at_row == 0, low_row, pltpu.roll(u, 1, 0))
    down = jnp.where(at_row == ROWS - 1, high_row, pltpu.roll(u, ROWS - 1, 0))
    left = jnp.where(at_lane == 0, low_col, pltpu.roll(u, 1, 1))
    right = jnp.where(at_lane == COLS - 1, high_col, pltpu.roll(u, COLS - 1, 1))
    return up, down, left, right


def span(back, front, limited):
    least = jnp.maximum(jnp.minimum(back, front), 0.0) + jnp.minimum(jnp.maximum(back, front), 0.0)
    return jnp.where(limited, least, 0.5 * (back + front))


def split_dot(x, tile):
    tile_high = tile.astype(jnp.bfloat16)
    tile_low = (tile - tile_high.astype(jnp.float32)).astype(jnp.bfloat16)
    x_high = x.astype(jnp.bfloat16).astype(jnp.float32)
    x_low = x - x_high
    left = jnp.concatenate([x_high, x_low], axis=0).astype(jnp.bfloat16)
    right = jnp.concatenate([x_high, jnp.zeros_like(x)], axis=0).astype(jnp.bfloat16)
    moving = jnp.concatenate([left, right], axis=1)
    held = jnp.concatenate([tile_high, tile_low], axis=1)
    out = lax.dot_general(
        moving, held, (((1,), (1,)), ((), ())), preferred_element_type=jnp.float32
    )
    return out[:PAD] + out[PAD:]


def stage_kernel(old, offsets_in, flags_in, own_in, x, own, cols, rows, offsets, flags, sems):
    copies = [
        pltpu.make_async_copy(held, here, sems.at[i])
        for i, (held, here) in enumerate(((offsets_in, offsets), (flags_in, flags), (own_in, own)))
    ]
    for copy in copies:
        copy.start()
    for f in range(FIELDS, PAD):
        x[pl.ds(f, BLOCKS, stride=PAD), :] = jnp.full(
            (BLOCKS, BLK), 1.0 if f == FIELDS else 0.0, jnp.float32
        )
    for copy in copies[:2]:
        copy.wait()
    limited = flags[...] > 0
    none = jnp.zeros((FIELDS, COLS), jnp.float32)
    none_col = jnp.zeros((ROWS, BLK), jnp.float32)
    for f in range(FIELDS):
        u = old[f]
        up, down, left, right = neighbours(u, f, (none, none), (none_col, none_col))
        rebuilt = (
            u
            + span(u - up, down - u, limited) * offsets[0]
            + span(u - left, right - u, limited) * offsets[1]
        )
        x[pl.ds(f, ROWS, stride=2 * PAD), :] = rebuilt[:, :BLK]
        x[pl.ds(PAD + f, ROWS, stride=2 * PAD), :] = rebuilt[:, BLK:]
    for side, (edge, beside) in enumerate(((0, 1), (COLS - 1, COLS - 2))):
        value, next_value = column(old, edge), column(old, beside)
        near, sign = value - next_value, (1.0, -1.0)[side]
        flag = flags[:, edge : edge + 1] > 0
        cols[side, 0] = value
        cols[side, 1] = -sign * near
        cols[side, 2] = span(sign * value, -sign * near, flag)
        cols[side, 3] = jnp.broadcast_to(offsets[1, :, edge : edge + 1], (ROWS, BLK))
        cols[side, 4] = jnp.broadcast_to(flags[:, edge : edge + 1], (ROWS, BLK)).astype(jnp.float32)
    for side, (edge, beside) in enumerate(((0, 1), (ROWS - 1, ROWS - 2))):
        value, next_value = old[:, edge, :], old[:, beside, :]
        near, sign = value - next_value, (1.0, -1.0)[side]
        flag = flags[edge : edge + 1, :] > 0
        rows[side, 0] = value
        rows[side, 1] = -sign * near
        rows[side, 2] = span(sign * value, -sign * near, flag)
        rows[side, 3] = jnp.broadcast_to(offsets[0, edge : edge + 1, :], (FIELDS, COLS))
        rows[side, 4] = jnp.broadcast_to(flags[edge : edge + 1, :], (FIELDS, COLS)).astype(jnp.float32)
    copies[2].wait()


def edge_change(ref, side, beyond):
    outer = ref[side, 0] - beyond if side == 0 else beyond - ref[side, 0]
    return (span(outer, ref[side, 1], ref[side, 4] > 0) - ref[side, 2]) * ref[side, 3]


def remap_kernel(
    source_in, dest_in, target_in, far_row, near_row, far_col, near_col, start_x, cols, rows, own,
    flux, parts, mass, source, dest, target, x, tiles, marks, sems, count, input_sems,
):
    inputs = [
        pltpu.make_async_copy(held, here, input_sems.at[i])
        for i, (held, here) in enumerate(((source_in, source), (dest_in, dest), (target_in, target)))
    ]
    for copy in inputs:
        copy.start()

    def tile_copy(c):
        span_of = pl.ds(c * CHUNK, CHUNK)
        return pltpu.make_async_copy(flux.at[span_of], tiles.at[span_of], sems.at[c])

    for c in range(TILES // CHUNK):
        tile_copy(c).start()
    x[...] = start_x[...]
    for side, beyond in enumerate(sides("sweep", near_row[:FIELDS, :], far_row[:FIELDS, :])):
        change = edge_change(rows, side, beyond)
        for h in range(2):
            at = pl.ds(((ROWS - 1) * side * 2 + h) * PAD, FIELDS)
            x[at, :] += change[:, h * BLK : (h + 1) * BLK]
    lanes = lane_of((ROWS, BLK))
    for side, beyond in enumerate(sides("cross", near_col[...], far_col[...])):
        change = edge_change(cols, side, beyond)
        for f in range(FIELDS):
            at = pl.ds(side * PAD + f, ROWS, stride=2 * PAD)
            x[at, :] += jnp.where(lanes == (BLK - 1) * side, change[:, f : f + 1], 0.0)
    marks[...] = jnp.full((SWEEPS, BLK), float(BLOCKS), jnp.float32)
    lanes = lane_of((1, BLK))

    def block(b):
        return x[pl.ds(pl.multiple_of(b * PAD, 8), PAD), :]

    def own_chunk(c, carry):
        first = c * CHUNK
        outs = [split_dot(block(first + k), own[first + k]) for k in range(CHUNK)]
        for k in range(CHUNK):
            mass[pl.ds(pl.multiple_of((first + k) * PAD, 8), PAD), :] = outs[k]
        return carry

    lax.fori_loop(0, BLOCKS // CHUNK, own_chunk, 0)
    for copy in inputs:
        copy.wait()
    for d in range(SWEEPS):
        count[d] = 0

    def flux_chunk(c, carry):
        tile_copy(c).wait()
        first = c * CHUNK
        outs = [split_dot(block(source[first + k]), tiles[first + k]) for k in range(CHUNK)]
        for k in range(CHUNK):
            d = dest[first + k]
            r = count[d]
            count[d] = r + 1
            parts[d, pl.ds(r * WIDE, WIDE), :] = outs[k][:WIDE]
            marks[pl.ds(d, 1), :] = jnp.where(
                lanes == r, target[first + k].astype(jnp.float32), marks[pl.ds(d, 1), :]
            )
        return carry

    lax.fori_loop(0, TILES // CHUNK, flux_chunk, 0)
    for d in range(SWEEPS):
        parts[d, pl.ds(SLOT_ROWS, 8), :] = jnp.broadcast_to(marks[d : d + 1, :], (8, BLK))


SUMS = 4


def receive_kernel(
    parts, mass, density, far_row, near_row, far_col, near_col, found, where, sem, *totals
):
    for s in range(SWEEPS):
        found[s : s + 1, :] = parts[s, SLOT_ROWS : SLOT_ROWS + 1, :].astype(jnp.int32)
    naming = pltpu.make_async_copy(found, where, sem)
    naming.start()
    totals[0][pl.ds(0, BLOCKS * PAD), :] = mass[...]
    for total in totals[1:]:
        total[...] = jnp.zeros(total.shape, jnp.float32)
    naming.wait()
    for s in range(SWEEPS):
        for k in range(0, CAP, SUMS):
            at = [pl.ds(pl.multiple_of(where[s, k + j] * PAD, 8), PAD) for j in range(SUMS)]
            old = [totals[j][at[j], :] for j in range(SUMS)]
            for j in range(SUMS):
                totals[j][at[j], :] = old[j] + parts[s, (k + j) * WIDE : (k + j) * WIDE + PAD, :]

    def field(h, f):
        at = pl.ds(h * PAD + f, ROWS, stride=2 * PAD)
        return sum(total[at, :] for total in totals)

    scale = [1.0 / field(h, FIELDS) for h in range(2)]
    for f in range(FIELDS):
        for h in range(2):
            density[f, :, h * BLK : (h + 1) * BLK] = field(h, f) * scale[h]
    pack_edges(density, odd("sweep"), odd("cross"), far_row, near_row, far_col, near_col)


def smooth_kernel(density, far_row, near_row, far_col, near_col, out):
    rows = sides("sweep", near_row[:FIELDS, :], far_row[:FIELDS, :])
    cols = sides("cross", near_col[...], far_col[...])
    for f in range(FIELDS):
        u = density[f]
        up, down, left, right = neighbours(u, f, rows, cols)
        out[f] = u + SMOOTHING * (up + down + left + right - 4.0 * u)


def in_place(held):
    return pltpu.with_memory_space_constraint(held, pltpu.HBM)


def params(mib):
    return pltpu.CompilerParams(vmem_limit_bytes=mib * 1024 * 1024)


def body(
    old_state, offsets, limiter_flags, self_tiles, flux_tiles, tile_source, tile_dest, tile_target
):
    vm, hbm = (pl.BlockSpec(memory_space=m) for m in (VMEM, pltpu.HBM))
    dma = pltpu.SemaphoreType.DMA
    shape = lambda *sizes: jax.ShapeDtypeStruct(sizes, jnp.float32)
    *edges, held = pl.pallas_call(
        edges_kernel, out_shape=EDGES + (shape(FIELDS, ROWS, COLS),), in_specs=[vm], out_specs=(vm,) * 5,
        input_output_aliases={0: 4}, compiler_params=params(16), name="edges",
    )(old_state)
    halos = exchange(*edges)
    start_x, own, cols, rows = pl.pallas_call(
        stage_kernel,
        out_shape=(
            shape(BLOCKS * PAD, BLK), shape(BLOCKS, BLK, BLK),
            shape(2, 5, ROWS, BLK), shape(2, 5, FIELDS, COLS),
        ),
        in_specs=[vm] + [hbm] * 3,
        out_specs=(vm,) * 4,
        scratch_shapes=[VMEM((2, ROWS, COLS), jnp.float32), VMEM((ROWS, COLS), jnp.int32), dma((3,))],
        compiler_params=params(16),
        cost_estimate=pl.CostEstimate(
            flops=40 * FIELDS * ROWS * COLS, bytes_accessed=BLOCKS * BLK * BLK * 4, transcendentals=0
        ),
        name="stage",
    )(held, in_place(offsets), in_place(limiter_flags), in_place(self_tiles))
    send, mass = pl.pallas_call(
        remap_kernel,
        out_shape=(shape(SWEEPS, PART_ROWS, BLK), shape(BLOCKS * PAD, BLK)),
        in_specs=[hbm] * 3 + [vm] * 8 + [hbm],
        out_specs=(vm, vm),
        scratch_shapes=[SMEM((TILES,), jnp.int32)] * 3
        + [
            VMEM((BLOCKS * PAD, BLK), jnp.float32),
            VMEM((TILES, BLK, BLK), jnp.float32),
            VMEM((SWEEPS, BLK), jnp.float32),
            dma((TILES // CHUNK,)),
            SMEM((SWEEPS,), jnp.int32),
            dma((3,)),
        ],
        compiler_params=params(32),
        cost_estimate=pl.CostEstimate(
            flops=2 * 6 * (TILES + BLOCKS) * PAD * BLK * BLK,
            bytes_accessed=TILES * BLK * BLK * 4,
            transcendentals=0,
        ),
        name="remap",
    )(
        *(in_place(held) for held in (tile_source, tile_dest.reshape(TILES), tile_target)),
        *halos, start_x, cols, rows, own, in_place(flux_tiles),
    )
    arrived = lax.all_to_all(send, "sweep", split_axis=0, concat_axis=0, tiled=True)
    density, *edges = pl.pallas_call(
        receive_kernel,
        out_shape=(jax.ShapeDtypeStruct((FIELDS, ROWS, COLS), jnp.float32),) + EDGES,
        in_specs=[vm, vm],
        out_specs=(vm,) * 5,
        scratch_shapes=[VMEM((SWEEPS, BLK), jnp.int32), SMEM((SWEEPS, BLK), jnp.int32), dma]
        + [VMEM(((BLOCKS + 1) * PAD, BLK), jnp.float32)] * SUMS,
        compiler_params=params(32),
        name="receive",
    )(arrived, mass)
    halos = exchange(*edges)
    return pl.pallas_call(
        smooth_kernel,
        out_shape=jax.ShapeDtypeStruct((FIELDS, ROWS, COLS), jnp.float32),
        in_specs=[vm] * 5,
        out_specs=vm,
        compiler_params=params(16),
        name="smooth",
    )(density, *halos)


def solution(mesh):
    placed = (
        P(None, "sweep", "cross"),
        P(None, "sweep", "cross"),
        P("sweep", "cross"),
        P(("sweep", "cross"), None, None),
        P(("sweep", "cross"), None, None),
        P(("sweep", "cross")),
        P(("sweep", "cross"), None),
        P(("sweep", "cross")),
    )
    return jax.shard_map(
        body, mesh=mesh, in_specs=placed, out_specs=P(None, "sweep", "cross"), check_vma=False
    )
```

```python
import functools

import jax
import jax.numpy as jnp
from jax import lax
from jax.experimental import pallas as pl
from jax.experimental.pallas import tpu as pltpu
from jax.sharding import PartitionSpec as P

SMOOTHING = 0.1
FIELDS, ROWS, COLS = 20, 48, 256
BLOCKS, BLK = 96, 128
TILES, CAP = 192, 24
SWEEPS, CROSSES = 16, 8
PAD = 24
EDGE_ROWS = 32
WIDE = FIELDS + 1
SLOT_ROWS = CAP * WIDE
PART_ROWS = SLOT_ROWS + 8
CHUNK = 48
VMEM = pltpu.VMEM
SMEM = pltpu.SMEM


def pairs(count, shift):
    return [(i, (((i + shift) ^ 1) - shift) % count) for i in range(count)]


def swap(values, axis, shift):
    return lax.ppermute(values, axis, pairs(lax.axis_size(axis), shift))


def lane_of(shape):
    return lax.broadcasted_iota(jnp.int32, shape, len(shape) - 1)


def row_of(shape):
    return lax.broadcasted_iota(jnp.int32, shape, len(shape) - 2)


def odd(axis):
    return lax.axis_index(axis) % 2 == 1


def packed(values_of):
    lanes = lane_of((ROWS, BLK))
    columns = jnp.zeros((ROWS, BLK), jnp.float32)
    for f in range(FIELDS):
        columns = jnp.where(lanes == f, values_of(f), columns)
    return columns


def column(ref, lane):
    return packed(lambda f: ref[f, :, lane : lane + 1])


def pack_edges(low_row, high_row, low_col, high_col, far_row, near_row, far_col, near_col):
    near_row[:FIELDS, :] = jnp.where(odd("sweep"), low_row, high_row)
    far_row[:FIELDS, :] = jnp.where(odd("sweep"), high_row, low_row)
    near_col[...] = jnp.where(odd("cross"), low_col, high_col)
    far_col[...] = jnp.where(odd("cross"), high_col, low_col)


def edges_kernel(
    old_in, offsets_in, flags_in, far_row, near_row, far_col, near_col, old, offsets, flags, sems
):
    copies = in_pieces(old_in, old, sems, GROUP)
    states = len(copies)
    copies += [
        pltpu.make_async_copy(offsets_in, offsets, sems.at[states]),
        pltpu.make_async_copy(flags_in, flags, sems.at[states + 1]),
    ]
    for copy in copies:
        copy.start()
    for copy in copies[:states]:
        copy.wait()
    pack_edges(
        old[:, 0, :], old[:, ROWS - 1, :], column(old, 0), column(old, COLS - 1),
        far_row, near_row, far_col, near_col,
    )
    for copy in copies[states:]:
        copy.wait()


EDGES = (
    jax.ShapeDtypeStruct((EDGE_ROWS, COLS), jnp.float32),
    jax.ShapeDtypeStruct((EDGE_ROWS, COLS), jnp.float32),
    jax.ShapeDtypeStruct((ROWS, BLK), jnp.float32),
    jax.ShapeDtypeStruct((ROWS, BLK), jnp.float32),
)


def exchange(far_row, near_row, far_col, near_col):
    return (
        swap(far_row, "sweep", 1),
        swap(near_row, "sweep", 0),
        swap(far_col, "cross", 1),
        swap(near_col, "cross", 0),
    )


def sides(axis, near, far):
    at, last = lax.axis_index(axis), lax.axis_size(axis) - 1
    before = jnp.where(at == 0, 0.0, jnp.where(odd(axis), near, far))
    after = jnp.where(at == last, 0.0, jnp.where(odd(axis), far, near))
    return before, after


def bare(u):
    at_row, at_lane = row_of((ROWS, COLS)), lane_of((ROWS, COLS))
    up = jnp.where(at_row == 0, 0.0, pltpu.roll(u, 1, 0))
    down = jnp.where(at_row == ROWS - 1, 0.0, pltpu.roll(u, ROWS - 1, 0))
    left = jnp.where(at_lane == 0, 0.0, pltpu.roll(u, 1, 1))
    right = jnp.where(at_lane == COLS - 1, 0.0, pltpu.roll(u, COLS - 1, 1))
    return up, down, left, right


def span(back, front, limited):
    least = jnp.maximum(jnp.minimum(back, front), 0.0) + jnp.minimum(jnp.maximum(back, front), 0.0)
    return jnp.where(limited, least, 0.5 * (back + front))


def split_dot(x, tile):
    tile_high = tile.astype(jnp.bfloat16)
    tile_low = (tile - tile_high.astype(jnp.float32)).astype(jnp.bfloat16)
    x_high = x.astype(jnp.bfloat16).astype(jnp.float32)
    x_low = x - x_high
    left = jnp.concatenate([x_high, x_low], axis=0).astype(jnp.bfloat16)
    right = jnp.concatenate([x_high, jnp.zeros_like(x)], axis=0).astype(jnp.bfloat16)
    moving = jnp.concatenate([left, right], axis=1)
    held = jnp.concatenate([tile_high, tile_low], axis=1)
    out = lax.dot_general(
        moving, held, (((1,), (1,)), ((), ())), preferred_element_type=jnp.float32
    )
    return out[:PAD] + out[PAD:]


def in_pieces(held, here, sems, size):
    parts = [pl.ds(i * size, size) for i in range(held.shape[0] // size)]
    return [
        pltpu.make_async_copy(held.at[part], here.at[part], sems.at[i])
        for i, part in enumerate(parts)
    ]


def stage_kernel(old, offsets, flags, own_in, x, own, cols, rows, sems):
    bring = in_pieces(own_in, own, sems, BLOCKS // PIECES)
    for piece in bring:
        piece.start()
    for f in range(FIELDS, PAD):
        x[pl.ds(f, BLOCKS, stride=PAD), :] = jnp.full(
            (BLOCKS, BLK), 1.0 if f == FIELDS else 0.0, jnp.float32
        )
    limited = flags[...] > 0

    def rebuild(f, carry):
        u = old[f]
        up, down, left, right = bare(u)
        rebuilt = (
            u
            + span(u - up, down - u, limited) * offsets[0]
            + span(u - left, right - u, limited) * offsets[1]
        )
        x[pl.ds(f, ROWS, stride=2 * PAD), :] = rebuilt[:, :BLK]
        x[pl.ds(PAD + f, ROWS, stride=2 * PAD), :] = rebuilt[:, BLK:]
        return carry

    lax.fori_loop(0, FIELDS, rebuild, 0, unroll=5)
    for side, (edge, beside) in enumerate(((0, 1), (COLS - 1, COLS - 2))):
        value, next_value = column(old, edge), column(old, beside)
        near, sign = value - next_value, (1.0, -1.0)[side]
        flag = flags[:, edge : edge + 1] > 0
        cols[side, 0] = value
        cols[side, 1] = -sign * near
        cols[side, 2] = span(sign * value, -sign * near, flag)
        cols[side, 3] = jnp.broadcast_to(offsets[1, :, edge : edge + 1], (ROWS, BLK))
        cols[side, 4] = jnp.broadcast_to(flags[:, edge : edge + 1], (ROWS, BLK)).astype(jnp.float32)
    for side, (edge, beside) in enumerate(((0, 1), (ROWS - 1, ROWS - 2))):
        value, next_value = old[:, edge, :], old[:, beside, :]
        near, sign = value - next_value, (1.0, -1.0)[side]
        flag = flags[edge : edge + 1, :] > 0
        rows[side, 0] = value
        rows[side, 1] = -sign * near
        rows[side, 2] = span(sign * value, -sign * near, flag)
        rows[side, 3] = jnp.broadcast_to(offsets[0, edge : edge + 1, :], (FIELDS, COLS))
        rows[side, 4] = jnp.broadcast_to(flags[edge : edge + 1, :], (FIELDS, COLS)).astype(jnp.float32)
    for piece in bring:
        piece.wait()


def edge_change(ref, side, beyond):
    outer = ref[side, 0] - beyond if side == 0 else beyond - ref[side, 0]
    return (span(outer, ref[side, 1], ref[side, 4] > 0) - ref[side, 2]) * ref[side, 3]


def remap_kernel(
    source_in, dest_in, target_in, far_row, near_row, far_col, near_col, start_x, cols, rows, own,
    flux, parts, mass, x, source, dest, target, tiles, marks, sems, count, input_sems,
):
    inputs = [
        pltpu.make_async_copy(held, here, input_sems.at[i])
        for i, (held, here) in enumerate(((source_in, source), (dest_in, dest), (target_in, target)))
    ]
    for copy in inputs:
        copy.start()

    def tile_copy(c):
        span_of = pl.ds(c * CHUNK, CHUNK)
        return pltpu.make_async_copy(flux.at[span_of], tiles.at[span_of], sems.at[c])

    for c in range(TILES // CHUNK):
        tile_copy(c).start()
    for side, beyond in enumerate(sides("sweep", near_row[:FIELDS, :], far_row[:FIELDS, :])):
        change = edge_change(rows, side, beyond)
        for h in range(2):
            at = pl.ds(((ROWS - 1) * side * 2 + h) * PAD, FIELDS)
            x[at, :] += change[:, h * BLK : (h + 1) * BLK]
    lanes = lane_of((ROWS, BLK))
    for side, beyond in enumerate(sides("cross", near_col[...], far_col[...])):
        change = edge_change(cols, side, beyond)
        for f in range(FIELDS):
            at = pl.ds(side * PAD + f, ROWS, stride=2 * PAD)
            x[at, :] += jnp.where(lanes == (BLK - 1) * side, change[:, f : f + 1], 0.0)
    marks[...] = jnp.full((SWEEPS, BLK), float(BLOCKS), jnp.float32)
    lanes = lane_of((1, BLK))

    def block(b):
        return x[pl.ds(pl.multiple_of(b * PAD, 8), PAD), :]

    def own_chunk(c, carry):
        first = c * CHUNK
        outs = [split_dot(block(first + k), own[first + k]) for k in range(CHUNK)]
        for k in range(CHUNK):
            mass[pl.ds(pl.multiple_of((first + k) * PAD, 8), PAD), :] = outs[k]
        return carry

    lax.fori_loop(0, BLOCKS // CHUNK, own_chunk, 0)
    for copy in inputs:
        copy.wait()
    for d in range(SWEEPS):
        count[d] = 0

    def flux_chunk(c, carry):
        tile_copy(c).wait()
        first = c * CHUNK
        outs = [split_dot(block(source[first + k]), tiles[first + k]) for k in range(CHUNK)]
        for k in range(CHUNK):
            d = dest[first + k]
            r = count[d]
            count[d] = r + 1
            parts[d, pl.ds(r * WIDE, WIDE), :] = outs[k][:WIDE]
            marks[pl.ds(d, 1), :] = jnp.where(
                lanes == r, target[first + k].astype(jnp.float32), marks[pl.ds(d, 1), :]
            )
        return carry

    lax.fori_loop(0, TILES // CHUNK, flux_chunk, 0)
    for d in range(SWEEPS):
        parts[d, pl.ds(SLOT_ROWS, 8), :] = jnp.broadcast_to(marks[d : d + 1, :], (8, BLK))


SUMS = 4
GROUP = 5
PIECES = 8


def receive_kernel(
    parts, mass, dense, far_row, near_row, far_col, near_col, found, where, sem, *totals
):
    for s in range(SWEEPS):
        found[s : s + 1, :] = parts[s, SLOT_ROWS : SLOT_ROWS + 1, :].astype(jnp.int32)
    naming = pltpu.make_async_copy(found, where, sem)
    naming.start()
    totals[0][pl.ds(0, BLOCKS * PAD), :] = mass[...]
    for total in totals[1:]:
        total[...] = jnp.zeros(total.shape, jnp.float32)
    naming.wait()
    for s in range(SWEEPS):
        for k in range(0, CAP, SUMS):
            at = [pl.ds(pl.multiple_of(where[s, k + j] * PAD, 8), PAD) for j in range(SUMS)]
            old = [totals[j][at[j], :] for j in range(SUMS)]
            for j in range(SUMS):
                totals[j][at[j], :] = old[j] + parts[s, (k + j) * WIDE : (k + j) * WIDE + PAD, :]

    for b in range(BLOCKS):
        at = pl.ds(b * PAD, PAD)
        value = sum(total[at, :] for total in totals)
        dense[at, :] = value * (1.0 / value[FIELDS:WIDE])

    def row(b):
        return jnp.concatenate(
            [dense[pl.ds((b + h) * PAD, FIELDS), :] for h in range(2)], axis=1
        )

    def col(h, lane):
        return packed(
            lambda f: dense[pl.ds(h * PAD + f, ROWS, stride=2 * PAD), :][:, lane : lane + 1]
        )

    pack_edges(
        row(0), row(BLOCKS - 2), col(0, 0), col(1, BLK - 1), far_row, near_row, far_col, near_col
    )


def inner_kernel(dense, out):
    for f in range(FIELDS):
        u = jnp.concatenate(
            [dense[pl.ds(h * PAD + f, ROWS, stride=2 * PAD), :] for h in range(2)], axis=1
        )
        up, down, left, right = bare(u)
        out[f] = u + SMOOTHING * (up + down + left + right - 4.0 * u)


def finish_kernel(inner, far_row, near_row, far_col, near_col, out, held, sems):
    low_row, high_row = sides("sweep", near_row[:FIELDS, :], far_row[:FIELDS, :])
    low_col, high_col = sides("cross", near_col[...], far_col[...])
    at_row, at_lane = row_of((ROWS, COLS)), lane_of((ROWS, COLS))
    copies = []
    for f in range(FIELDS):
        beyond = (
            jnp.where(at_row == 0, low_row[f : f + 1, :], 0.0)
            + jnp.where(at_row == ROWS - 1, high_row[f : f + 1, :], 0.0)
            + jnp.where(at_lane == 0, low_col[:, f : f + 1], 0.0)
            + jnp.where(at_lane == COLS - 1, high_col[:, f : f + 1], 0.0)
        )
        held[f] = inner[f] + SMOOTHING * beyond
        if f % GROUP == GROUP - 1:
            group = pl.ds(f + 1 - GROUP, GROUP)
            copies.append(
                pltpu.make_async_copy(held.at[group], out.at[group], sems.at[f // GROUP])
            )
            copies[-1].start()
    for copy in copies:
        copy.wait()


def in_place(held):
    return pltpu.with_memory_space_constraint(held, pltpu.HBM)


def params(mib):
    return pltpu.CompilerParams(vmem_limit_bytes=mib * 1024 * 1024)


def body(
    old_state, offsets, limiter_flags, self_tiles, flux_tiles, tile_source, tile_dest, tile_target
):
    vm, hbm = (pl.BlockSpec(memory_space=m) for m in (VMEM, pltpu.HBM))
    dma = pltpu.SemaphoreType.DMA
    shape = lambda *sizes: jax.ShapeDtypeStruct(sizes, jnp.float32)
    *edges, old, shifts, flags = pl.pallas_call(
        edges_kernel,
        out_shape=EDGES
        + (
            shape(FIELDS, ROWS, COLS), shape(2, ROWS, COLS),
            jax.ShapeDtypeStruct((ROWS, COLS), jnp.int32),
        ),
        in_specs=[hbm] * 3,
        out_specs=(vm,) * 7,
        scratch_shapes=[dma((FIELDS // GROUP + 2,))],
        compiler_params=params(16),
        name="edges",
    )(in_place(old_state), in_place(offsets), in_place(limiter_flags))
    halos = exchange(*edges)
    start_x, own, cols, rows = pl.pallas_call(
        stage_kernel,
        out_shape=(
            shape(BLOCKS * PAD, BLK), shape(BLOCKS, BLK, BLK),
            shape(2, 5, ROWS, BLK), shape(2, 5, FIELDS, COLS),
        ),
        in_specs=[vm] * 3 + [hbm],
        out_specs=(vm,) * 4,
        scratch_shapes=[dma((PIECES,))],
        compiler_params=params(16),
        cost_estimate=pl.CostEstimate(
            flops=40 * FIELDS * ROWS * COLS, bytes_accessed=BLOCKS * BLK * BLK * 4, transcendentals=0
        ),
        name="stage",
    )(old, shifts, flags, in_place(self_tiles))
    send, mass, _ = pl.pallas_call(
        remap_kernel,
        out_shape=(shape(SWEEPS, PART_ROWS, BLK), shape(BLOCKS * PAD, BLK), shape(BLOCKS * PAD, BLK)),
        in_specs=[hbm] * 3 + [vm] * 8 + [hbm],
        out_specs=(vm,) * 3,
        input_output_aliases={7: 2},
        scratch_shapes=[SMEM((TILES,), jnp.int32)] * 3
        + [
            VMEM((TILES, BLK, BLK), jnp.float32),
            VMEM((SWEEPS, BLK), jnp.float32),
            dma((TILES // CHUNK,)),
            SMEM((SWEEPS,), jnp.int32),
            dma((3,)),
        ],
        compiler_params=params(32),
        cost_estimate=pl.CostEstimate(
            flops=2 * 6 * (TILES + BLOCKS) * PAD * BLK * BLK,
            bytes_accessed=TILES * BLK * BLK * 4,
            transcendentals=0,
        ),
        name="remap",
    )(
        *(in_place(held) for held in (tile_source, tile_dest.reshape(TILES), tile_target)),
        *halos, start_x, cols, rows, own, in_place(flux_tiles),
    )
    arrived = lax.all_to_all(send, "sweep", split_axis=0, concat_axis=0, tiled=True)
    dense, *edges = pl.pallas_call(
        receive_kernel,
        out_shape=(shape(BLOCKS * PAD, BLK),) + EDGES,
        in_specs=[vm, vm],
        out_specs=(vm,) * 5,
        scratch_shapes=[VMEM((SWEEPS, BLK), jnp.int32), SMEM((SWEEPS, BLK), jnp.int32), dma]
        + [VMEM(((BLOCKS + 1) * PAD, BLK), jnp.float32)] * SUMS,
        compiler_params=params(32),
        name="receive",
    )(arrived, mass)
    halos = exchange(*edges)
    inner = pl.pallas_call(
        inner_kernel,
        out_shape=shape(FIELDS, ROWS, COLS),
        in_specs=[vm],
        out_specs=vm,
        compiler_params=params(16),
        cost_estimate=pl.CostEstimate(
            flops=20 * FIELDS * ROWS * COLS, bytes_accessed=8 * FIELDS * ROWS * COLS, transcendentals=0
        ),
        name="inner",
    )(dense)
    return pl.pallas_call(
        finish_kernel,
        out_shape=shape(FIELDS, ROWS, COLS),
        in_specs=[vm] * 5,
        out_specs=hbm,
        scratch_shapes=[VMEM((FIELDS, ROWS, COLS), jnp.float32), dma((FIELDS // GROUP,))],
        compiler_params=params(16),
        name="finish",
    )(inner, *halos)


def solution(mesh):
    placed = (
        P(None, "sweep", "cross"),
        P(None, "sweep", "cross"),
        P("sweep", "cross"),
        P(("sweep", "cross"), None, None),
        P(("sweep", "cross"), None, None),
        P(("sweep", "cross")),
        P(("sweep", "cross"), None),
        P(("sweep", "cross")),
    )
    return jax.shard_map(
        body, mesh=mesh, in_specs=placed, out_specs=P(None, "sweep", "cross"), check_vma=False
    )
```

```python
import functools

import jax
import jax.numpy as jnp
from jax import lax
from jax.experimental import pallas as pl
from jax.experimental.pallas import tpu as pltpu
from jax.sharding import PartitionSpec as P

SMOOTHING = 0.1
FIELDS, ROWS, COLS = 20, 48, 256
BLOCKS, BLK = 96, 128
TILES, CAP = 192, 24
SWEEPS, CROSSES = 16, 8
PAD = 24
EDGE_ROWS = 32
WIDE = FIELDS + 1
SLOT_ROWS = CAP * WIDE
PART_ROWS = SLOT_ROWS + 8
CHUNK = 48
VMEM = pltpu.VMEM
SMEM = pltpu.SMEM


def pairs(count, shift):
    return [(i, (((i + shift) ^ 1) - shift) % count) for i in range(count)]


def swap(values, axis, shift):
    return lax.ppermute(values, axis, pairs(lax.axis_size(axis), shift))


def lane_of(shape):
    return lax.broadcasted_iota(jnp.int32, shape, len(shape) - 1)


def row_of(shape):
    return lax.broadcasted_iota(jnp.int32, shape, len(shape) - 2)


def odd(axis):
    return lax.axis_index(axis) % 2 == 1


def packed(values_of):
    lanes = lane_of((ROWS, BLK))
    columns = jnp.zeros((ROWS, BLK), jnp.float32)
    for f in range(FIELDS):
        columns = jnp.where(lanes == f, values_of(f), columns)
    return columns


def column(ref, lane):
    return packed(lambda f: ref[f, :, lane : lane + 1])


def pack_edges(low_row, high_row, low_col, high_col, far_row, near_row, far_col, near_col):
    near_row[:FIELDS, :] = jnp.where(odd("sweep"), low_row, high_row)
    far_row[:FIELDS, :] = jnp.where(odd("sweep"), high_row, low_row)
    near_col[...] = jnp.where(odd("cross"), low_col, high_col)
    far_col[...] = jnp.where(odd("cross"), high_col, low_col)


def edges_kernel(
    old_in, offsets_in, flags_in, own_in, far_row, near_row, far_col, near_col, old, offsets, flags, own,
    sems,
):
    copies = in_pieces(old_in, old, sems, GROUP)
    states = len(copies)
    copies += [
        pltpu.make_async_copy(offsets_in, offsets, sems.at[states]),
        pltpu.make_async_copy(flags_in, flags, sems.at[states + 1]),
        pltpu.make_async_copy(own_in.at[pl.ds(0, EARLY)], own.at[pl.ds(0, EARLY)], sems.at[states + 2]),
    ]
    for copy in copies:
        copy.start()
    for copy in copies[:states]:
        copy.wait()
    pack_edges(
        old[:, 0, :], old[:, ROWS - 1, :], column(old, 0), column(old, COLS - 1),
        far_row, near_row, far_col, near_col,
    )
    for copy in copies[states:]:
        copy.wait()


EDGES = (
    jax.ShapeDtypeStruct((EDGE_ROWS, COLS), jnp.float32),
    jax.ShapeDtypeStruct((EDGE_ROWS, COLS), jnp.float32),
    jax.ShapeDtypeStruct((ROWS, BLK), jnp.float32),
    jax.ShapeDtypeStruct((ROWS, BLK), jnp.float32),
)


def exchange(far_row, near_row, far_col, near_col):
    return (
        swap(far_row, "sweep", 1),
        swap(near_row, "sweep", 0),
        swap(far_col, "cross", 1),
        swap(near_col, "cross", 0),
    )


def sides(axis, near, far):
    at, last = lax.axis_index(axis), lax.axis_size(axis) - 1
    before = jnp.where(at == 0, 0.0, jnp.where(odd(axis), near, far))
    after = jnp.where(at == last, 0.0, jnp.where(odd(axis), far, near))
    return before, after


def bare(u):
    at_row, at_lane = row_of((ROWS, COLS)), lane_of((ROWS, COLS))
    up = jnp.where(at_row == 0, 0.0, pltpu.roll(u, 1, 0))
    down = jnp.where(at_row == ROWS - 1, 0.0, pltpu.roll(u, ROWS - 1, 0))
    left = jnp.where(at_lane == 0, 0.0, pltpu.roll(u, 1, 1))
    right = jnp.where(at_lane == COLS - 1, 0.0, pltpu.roll(u, COLS - 1, 1))
    return up, down, left, right


def span(back, front, limited):
    least = jnp.maximum(jnp.minimum(back, front), 0.0) + jnp.minimum(jnp.maximum(back, front), 0.0)
    return jnp.where(limited, least, 0.5 * (back + front))


def split_dot(x, tile):
    tile_high = tile.astype(jnp.bfloat16)
    tile_low = (tile - tile_high.astype(jnp.float32)).astype(jnp.bfloat16)
    x_high = x.astype(jnp.bfloat16).astype(jnp.float32)
    x_low = x - x_high
    left = jnp.concatenate([x_high, x_low], axis=0).astype(jnp.bfloat16)
    right = jnp.concatenate([x_high, jnp.zeros_like(x)], axis=0).astype(jnp.bfloat16)
    moving = jnp.concatenate([left, right], axis=1)
    held = jnp.concatenate([tile_high, tile_low], axis=1)
    out = lax.dot_general(
        moving, held, (((1,), (1,)), ((), ())), preferred_element_type=jnp.float32
    )
    return out[:PAD] + out[PAD:]


def in_pieces(held, here, sems, size):
    parts = [pl.ds(i * size, size) for i in range(held.shape[0] // size)]
    return [
        pltpu.make_async_copy(held.at[part], here.at[part], sems.at[i])
        for i, part in enumerate(parts)
    ]


def stage_kernel(old, offsets, flags, own_in, begun, x, own, cols, rows, sems):
    rest = pl.ds(EARLY, BLOCKS - EARLY)
    bring = in_pieces(own_in.at[rest], own.at[rest], sems, (BLOCKS - EARLY) // PIECES)
    for piece in bring:
        piece.start()
    for f in range(FIELDS, PAD):
        x[pl.ds(f, BLOCKS, stride=PAD), :] = jnp.full(
            (BLOCKS, BLK), 1.0 if f == FIELDS else 0.0, jnp.float32
        )
    limited = flags[...] > 0

    def rebuild(f, carry):
        u = old[f]
        up, down, left, right = bare(u)
        rebuilt = (
            u
            + span(u - up, down - u, limited) * offsets[0]
            + span(u - left, right - u, limited) * offsets[1]
        )
        x[pl.ds(f, ROWS, stride=2 * PAD), :] = rebuilt[:, :BLK]
        x[pl.ds(PAD + f, ROWS, stride=2 * PAD), :] = rebuilt[:, BLK:]
        return carry

    lax.fori_loop(0, FIELDS, rebuild, 0, unroll=5)
    for side, (edge, beside) in enumerate(((0, 1), (COLS - 1, COLS - 2))):
        value, next_value = column(old, edge), column(old, beside)
        near, sign = value - next_value, (1.0, -1.0)[side]
        flag = flags[:, edge : edge + 1] > 0
        cols[side, 0] = value
        cols[side, 1] = -sign * near
        cols[side, 2] = span(sign * value, -sign * near, flag)
        cols[side, 3] = jnp.broadcast_to(offsets[1, :, edge : edge + 1], (ROWS, BLK))
        cols[side, 4] = jnp.broadcast_to(flags[:, edge : edge + 1], (ROWS, BLK)).astype(jnp.float32)
    for side, (edge, beside) in enumerate(((0, 1), (ROWS - 1, ROWS - 2))):
        value, next_value = old[:, edge, :], old[:, beside, :]
        near, sign = value - next_value, (1.0, -1.0)[side]
        flag = flags[edge : edge + 1, :] > 0
        rows[side, 0] = value
        rows[side, 1] = -sign * near
        rows[side, 2] = span(sign * value, -sign * near, flag)
        rows[side, 3] = jnp.broadcast_to(offsets[0, edge : edge + 1, :], (FIELDS, COLS))
        rows[side, 4] = jnp.broadcast_to(flags[edge : edge + 1, :], (FIELDS, COLS)).astype(jnp.float32)
    for piece in bring:
        piece.wait()


def edge_change(ref, side, beyond):
    outer = ref[side, 0] - beyond if side == 0 else beyond - ref[side, 0]
    return (span(outer, ref[side, 1], ref[side, 4] > 0) - ref[side, 2]) * ref[side, 3]


def remap_kernel(
    source_in, dest_in, target_in, far_row, near_row, far_col, near_col, start_x, cols, rows, own,
    flux, parts, mass, x, source, dest, target, tiles, marks, sems, count, input_sems,
):
    inputs = [
        pltpu.make_async_copy(held, here, input_sems.at[i])
        for i, (held, here) in enumerate(((source_in, source), (dest_in, dest), (target_in, target)))
    ]
    for copy in inputs:
        copy.start()

    def tile_copy(c):
        span_of = pl.ds(c * CHUNK, CHUNK)
        return pltpu.make_async_copy(flux.at[span_of], tiles.at[span_of], sems.at[c])

    for c in range(TILES // CHUNK):
        tile_copy(c).start()
    for side, beyond in enumerate(sides("sweep", near_row[:FIELDS, :], far_row[:FIELDS, :])):
        change = edge_change(rows, side, beyond)
        for h in range(2):
            at = pl.ds(((ROWS - 1) * side * 2 + h) * PAD, FIELDS)
            x[at, :] += change[:, h * BLK : (h + 1) * BLK]
    lanes = lane_of((ROWS, BLK))
    for side, beyond in enumerate(sides("cross", near_col[...], far_col[...])):
        change = edge_change(cols, side, beyond)
        for f in range(FIELDS):
            at = pl.ds(side * PAD + f, ROWS, stride=2 * PAD)
            x[at, :] += jnp.where(lanes == (BLK - 1) * side, change[:, f : f + 1], 0.0)
    marks[...] = jnp.full((SWEEPS, BLK), float(BLOCKS), jnp.float32)
    lanes = lane_of((1, BLK))

    def block(b):
        return x[pl.ds(pl.multiple_of(b * PAD, 8), PAD), :]

    def own_chunk(c, carry):
        first = c * CHUNK
        outs = [split_dot(block(first + k), own[first + k]) for k in range(CHUNK)]
        for k in range(CHUNK):
            mass[pl.ds(pl.multiple_of((first + k) * PAD, 8), PAD), :] = outs[k]
        return carry

    lax.fori_loop(0, BLOCKS // CHUNK, own_chunk, 0)
    for copy in inputs:
        copy.wait()
    for d in range(SWEEPS):
        count[d] = 0

    def flux_chunk(c, carry):
        tile_copy(c).wait()
        first = c * CHUNK
        outs = [split_dot(block(source[first + k]), tiles[first + k]) for k in range(CHUNK)]
        for k in range(CHUNK):
            d = dest[first + k]
            r = count[d]
            count[d] = r + 1
            parts[d, pl.ds(r * WIDE, WIDE), :] = outs[k][:WIDE]
            marks[pl.ds(d, 1), :] = jnp.where(
                lanes == r, target[first + k].astype(jnp.float32), marks[pl.ds(d, 1), :]
            )
        return carry

    lax.fori_loop(0, TILES // CHUNK, flux_chunk, 0)
    for d in range(SWEEPS):
        parts[d, pl.ds(SLOT_ROWS, 8), :] = jnp.broadcast_to(marks[d : d + 1, :], (8, BLK))


SUMS = 4
GROUP = 5
PIECES = 8
EARLY = 32


def receive_kernel(
    parts, mass, dense, far_row, near_row, far_col, near_col, found, where, sem, *totals
):
    for s in range(SWEEPS):
        found[s : s + 1, :] = parts[s, SLOT_ROWS : SLOT_ROWS + 1, :].astype(jnp.int32)
    naming = pltpu.make_async_copy(found, where, sem)
    naming.start()
    totals[0][pl.ds(0, BLOCKS * PAD), :] = mass[...]
    for total in totals[1:]:
        total[...] = jnp.zeros(total.shape, jnp.float32)
    naming.wait()
    for s in range(SWEEPS):
        for k in range(0, CAP, SUMS):
            at = [pl.ds(pl.multiple_of(where[s, k + j] * PAD, 8), PAD) for j in range(SUMS)]
            old = [totals[j][at[j], :] for j in range(SUMS)]
            for j in range(SUMS):
                totals[j][at[j], :] = old[j] + parts[s, (k + j) * WIDE : (k + j) * WIDE + PAD, :]

    for b in range(BLOCKS):
        at = pl.ds(b * PAD, PAD)
        value = sum(total[at, :] for total in totals)
        dense[at, :] = value * (1.0 / value[FIELDS:WIDE])

    def row(b):
        return jnp.concatenate(
            [dense[pl.ds((b + h) * PAD, FIELDS), :] for h in range(2)], axis=1
        )

    def col(h, lane):
        return packed(
            lambda f: dense[pl.ds(h * PAD + f, ROWS, stride=2 * PAD), :][:, lane : lane + 1]
        )

    pack_edges(
        row(0), row(BLOCKS - 2), col(0, 0), col(1, BLK - 1), far_row, near_row, far_col, near_col
    )


def inner_kernel(dense, out):
    for f in range(FIELDS):
        u = jnp.concatenate(
            [dense[pl.ds(h * PAD + f, ROWS, stride=2 * PAD), :] for h in range(2)], axis=1
        )
        up, down, left, right = bare(u)
        out[f] = u + SMOOTHING * (up + down + left + right - 4.0 * u)


def finish_kernel(inner, far_row, near_row, far_col, near_col, out, held, sems):
    low_row, high_row = sides("sweep", near_row[:FIELDS, :], far_row[:FIELDS, :])
    low_col, high_col = sides("cross", near_col[...], far_col[...])
    at_row, at_lane = row_of((ROWS, COLS)), lane_of((ROWS, COLS))
    copies = []
    for f in range(FIELDS):
        beyond = (
            jnp.where(at_row == 0, low_row[f : f + 1, :], 0.0)
            + jnp.where(at_row == ROWS - 1, high_row[f : f + 1, :], 0.0)
            + jnp.where(at_lane == 0, low_col[:, f : f + 1], 0.0)
            + jnp.where(at_lane == COLS - 1, high_col[:, f : f + 1], 0.0)
        )
        held[f] = inner[f] + SMOOTHING * beyond
        if f % GROUP == GROUP - 1:
            group = pl.ds(f + 1 - GROUP, GROUP)
            copies.append(
                pltpu.make_async_copy(held.at[group], out.at[group], sems.at[f // GROUP])
            )
            copies[-1].start()
    for copy in copies:
        copy.wait()


def in_place(held):
    return pltpu.with_memory_space_constraint(held, pltpu.HBM)


def params(mib):
    return pltpu.CompilerParams(vmem_limit_bytes=mib * 1024 * 1024)


def body(
    old_state, offsets, limiter_flags, self_tiles, flux_tiles, tile_source, tile_dest, tile_target
):
    vm, hbm = (pl.BlockSpec(memory_space=m) for m in (VMEM, pltpu.HBM))
    dma = pltpu.SemaphoreType.DMA
    shape = lambda *sizes: jax.ShapeDtypeStruct(sizes, jnp.float32)
    *edges, old, shifts, flags, own = pl.pallas_call(
        edges_kernel,
        out_shape=EDGES
        + (
            shape(FIELDS, ROWS, COLS), shape(2, ROWS, COLS),
            jax.ShapeDtypeStruct((ROWS, COLS), jnp.int32), shape(BLOCKS, BLK, BLK),
        ),
        in_specs=[hbm] * 4,
        out_specs=(vm,) * 8,
        scratch_shapes=[dma((FIELDS // GROUP + 3,))],
        compiler_params=params(16),
        name="edges",
    )(in_place(old_state), in_place(offsets), in_place(limiter_flags), in_place(self_tiles))
    halos = exchange(*edges)
    start_x, own, cols, rows = pl.pallas_call(
        stage_kernel,
        out_shape=(
            shape(BLOCKS * PAD, BLK), shape(BLOCKS, BLK, BLK),
            shape(2, 5, ROWS, BLK), shape(2, 5, FIELDS, COLS),
        ),
        in_specs=[vm] * 3 + [hbm, vm],
        out_specs=(vm,) * 4,
        input_output_aliases={4: 1},
        scratch_shapes=[dma((PIECES,))],
        compiler_params=params(16),
        cost_estimate=pl.CostEstimate(
            flops=40 * FIELDS * ROWS * COLS, bytes_accessed=BLOCKS * BLK * BLK * 4, transcendentals=0
        ),
        name="stage",
    )(old, shifts, flags, in_place(self_tiles), own)
    send, mass, _ = pl.pallas_call(
        remap_kernel,
        out_shape=(shape(SWEEPS, PART_ROWS, BLK), shape(BLOCKS * PAD, BLK), shape(BLOCKS * PAD, BLK)),
        in_specs=[hbm] * 3 + [vm] * 8 + [hbm],
        out_specs=(vm,) * 3,
        input_output_aliases={7: 2},
        scratch_shapes=[SMEM((TILES,), jnp.int32)] * 3
        + [
            VMEM((TILES, BLK, BLK), jnp.float32),
            VMEM((SWEEPS, BLK), jnp.float32),
            dma((TILES // CHUNK,)),
            SMEM((SWEEPS,), jnp.int32),
            dma((3,)),
        ],
        compiler_params=params(32),
        cost_estimate=pl.CostEstimate(
            flops=2 * 6 * (TILES + BLOCKS) * PAD * BLK * BLK,
            bytes_accessed=TILES * BLK * BLK * 4,
            transcendentals=0,
        ),
        name="remap",
    )(
        *(in_place(held) for held in (tile_source, tile_dest.reshape(TILES), tile_target)),
        *halos, start_x, cols, rows, own, in_place(flux_tiles),
    )
    arrived = lax.all_to_all(send, "sweep", split_axis=0, concat_axis=0, tiled=True)
    dense, *edges = pl.pallas_call(
        receive_kernel,
        out_shape=(shape(BLOCKS * PAD, BLK),) + EDGES,
        in_specs=[vm, vm],
        out_specs=(vm,) * 5,
        scratch_shapes=[VMEM((SWEEPS, BLK), jnp.int32), SMEM((SWEEPS, BLK), jnp.int32), dma]
        + [VMEM(((BLOCKS + 1) * PAD, BLK), jnp.float32)] * SUMS,
        compiler_params=params(32),
        name="receive",
    )(arrived, mass)
    halos = exchange(*edges)
    inner = pl.pallas_call(
        inner_kernel,
        out_shape=shape(FIELDS, ROWS, COLS),
        in_specs=[vm],
        out_specs=vm,
        compiler_params=params(16),
        cost_estimate=pl.CostEstimate(
            flops=20 * FIELDS * ROWS * COLS, bytes_accessed=8 * FIELDS * ROWS * COLS, transcendentals=0
        ),
        name="inner",
    )(dense)
    return pl.pallas_call(
        finish_kernel,
        out_shape=shape(FIELDS, ROWS, COLS),
        in_specs=[vm] * 5,
        out_specs=hbm,
        scratch_shapes=[VMEM((FIELDS, ROWS, COLS), jnp.float32), dma((FIELDS // GROUP,))],
        compiler_params=params(16),
        name="finish",
    )(inner, *halos)


def solution(mesh):
    placed = (
        P(None, "sweep", "cross"),
        P(None, "sweep", "cross"),
        P("sweep", "cross"),
        P(("sweep", "cross"), None, None),
        P(("sweep", "cross"), None, None),
        P(("sweep", "cross")),
        P(("sweep", "cross"), None),
        P(("sweep", "cross")),
    )
    return jax.shard_map(
        body, mesh=mesh, in_specs=placed, out_specs=P(None, "sweep", "cross"), check_vma=False
    )
```

```python
import functools

import jax
import jax.numpy as jnp
from jax import lax
from jax.experimental import pallas as pl
from jax.experimental.pallas import tpu as pltpu
from jax.sharding import PartitionSpec as P

SMOOTHING = 0.1
FIELDS, ROWS, COLS = 20, 48, 256
BLOCKS, BLK = 96, 128
TILES, CAP = 192, 24
SWEEPS, CROSSES = 16, 8
PAD = 24
EDGE_ROWS = 32
WIDE = FIELDS + 1
SLOT_ROWS = CAP * WIDE
PART_ROWS = SLOT_ROWS + 8
CHUNK = 48
VMEM = pltpu.VMEM
SMEM = pltpu.SMEM


def pairs(count, shift):
    return [(i, (((i + shift) ^ 1) - shift) % count) for i in range(count)]


def swap(values, axis, shift):
    return lax.ppermute(values, axis, pairs(lax.axis_size(axis), shift))


def lane_of(shape):
    return lax.broadcasted_iota(jnp.int32, shape, len(shape) - 1)


def row_of(shape):
    return lax.broadcasted_iota(jnp.int32, shape, len(shape) - 2)


def odd(axis):
    return lax.axis_index(axis) % 2 == 1


def packed(values_of):
    lanes = lane_of((ROWS, BLK))
    columns = jnp.zeros((ROWS, BLK), jnp.float32)
    for f in range(FIELDS):
        columns = jnp.where(lanes == f, values_of(f), columns)
    return columns


def column(ref, lane):
    return packed(lambda f: ref[f, :, lane : lane + 1])


def pack_edges(low_row, high_row, low_col, high_col, far_row, near_row, far_col, near_col):
    near_row[:FIELDS, :] = jnp.where(odd("sweep"), low_row, high_row)
    far_row[:FIELDS, :] = jnp.where(odd("sweep"), high_row, low_row)
    near_col[...] = jnp.where(odd("cross"), low_col, high_col)
    far_col[...] = jnp.where(odd("cross"), high_col, low_col)


def edges_kernel(
    old_in, offsets_in, flags_in, own_in, far_row, near_row, far_col, near_col, old, offsets, flags, own,
    sems,
):
    copies = in_pieces(old_in, old, sems, GROUP)
    states = len(copies)
    copies += [
        pltpu.make_async_copy(offsets_in, offsets, sems.at[states]),
        pltpu.make_async_copy(flags_in, flags, sems.at[states + 1]),
        pltpu.make_async_copy(own_in.at[pl.ds(0, EARLY)], own.at[pl.ds(0, EARLY)], sems.at[states + 2]),
    ]
    for copy in copies:
        copy.start()
    for copy in copies[:states]:
        copy.wait()
    pack_edges(
        old[:, 0, :], old[:, ROWS - 1, :], column(old, 0), column(old, COLS - 1),
        far_row, near_row, far_col, near_col,
    )
    for copy in copies[states:]:
        copy.wait()


EDGES = (
    jax.ShapeDtypeStruct((EDGE_ROWS, COLS), jnp.float32),
    jax.ShapeDtypeStruct((EDGE_ROWS, COLS), jnp.float32),
    jax.ShapeDtypeStruct((ROWS, BLK), jnp.float32),
    jax.ShapeDtypeStruct((ROWS, BLK), jnp.float32),
)


def exchange(far_row, near_row, far_col, near_col):
    return (
        swap(far_row, "sweep", 1),
        swap(near_row, "sweep", 0),
        swap(far_col, "cross", 1),
        swap(near_col, "cross", 0),
    )


def sides(axis, near, far):
    at, last = lax.axis_index(axis), lax.axis_size(axis) - 1
    before = jnp.where(at == 0, 0.0, jnp.where(odd(axis), near, far))
    after = jnp.where(at == last, 0.0, jnp.where(odd(axis), far, near))
    return before, after


def bare(u):
    at_row, at_lane = row_of((ROWS, COLS)), lane_of((ROWS, COLS))
    up = jnp.where(at_row == 0, 0.0, pltpu.roll(u, 1, 0))
    down = jnp.where(at_row == ROWS - 1, 0.0, pltpu.roll(u, ROWS - 1, 0))
    left = jnp.where(at_lane == 0, 0.0, pltpu.roll(u, 1, 1))
    right = jnp.where(at_lane == COLS - 1, 0.0, pltpu.roll(u, COLS - 1, 1))
    return up, down, left, right


def span(back, front, limited):
    least = jnp.maximum(jnp.minimum(back, front), 0.0) + jnp.minimum(jnp.maximum(back, front), 0.0)
    return jnp.where(limited, least, 0.5 * (back + front))


def split_dot(x, tile):
    tile_high = tile.astype(jnp.bfloat16)
    tile_low = (tile - tile_high.astype(jnp.float32)).astype(jnp.bfloat16)
    x_high = x.astype(jnp.bfloat16).astype(jnp.float32)
    x_low = x - x_high
    left = jnp.concatenate([x_high, x_low], axis=0).astype(jnp.bfloat16)
    right = jnp.concatenate([x_high, jnp.zeros_like(x)], axis=0).astype(jnp.bfloat16)
    moving = jnp.concatenate([left, right], axis=1)
    held = jnp.concatenate([tile_high, tile_low], axis=1)
    out = lax.dot_general(
        moving, held, (((1,), (1,)), ((), ())), preferred_element_type=jnp.float32
    )
    return out[:PAD] + out[PAD:]


def in_pieces(held, here, sems, size):
    parts = [pl.ds(i * size, size) for i in range(held.shape[0] // size)]
    return [
        pltpu.make_async_copy(held.at[part], here.at[part], sems.at[i])
        for i, part in enumerate(parts)
    ]


def stage_kernel(old, offsets, flags, own_in, begun, x, own, cols, rows, sems):
    rest = pl.ds(EARLY, BLOCKS - EARLY)
    bring = in_pieces(own_in.at[rest], own.at[rest], sems, (BLOCKS - EARLY) // PIECES)
    for piece in bring:
        piece.start()
    for f in range(FIELDS, PAD):
        x[pl.ds(f, BLOCKS, stride=PAD), :] = jnp.full(
            (BLOCKS, BLK), 1.0 if f == FIELDS else 0.0, jnp.float32
        )
    limited = flags[...] > 0

    def rebuild(f, carry):
        u = old[f]
        up, down, left, right = bare(u)
        rebuilt = (
            u
            + span(u - up, down - u, limited) * offsets[0]
            + span(u - left, right - u, limited) * offsets[1]
        )
        x[pl.ds(f, ROWS, stride=2 * PAD), :] = rebuilt[:, :BLK]
        x[pl.ds(PAD + f, ROWS, stride=2 * PAD), :] = rebuilt[:, BLK:]
        return carry

    lax.fori_loop(0, FIELDS, rebuild, 0, unroll=5)
    for side, (edge, beside) in enumerate(((0, 1), (COLS - 1, COLS - 2))):
        value, next_value = column(old, edge), column(old, beside)
        near, sign = value - next_value, (1.0, -1.0)[side]
        flag = flags[:, edge : edge + 1] > 0
        cols[side, 0] = value
        cols[side, 1] = -sign * near
        cols[side, 2] = span(sign * value, -sign * near, flag)
        cols[side, 3] = jnp.broadcast_to(offsets[1, :, edge : edge + 1], (ROWS, BLK))
        cols[side, 4] = jnp.broadcast_to(flags[:, edge : edge + 1], (ROWS, BLK)).astype(jnp.float32)
    for side, (edge, beside) in enumerate(((0, 1), (ROWS - 1, ROWS - 2))):
        value, next_value = old[:, edge, :], old[:, beside, :]
        near, sign = value - next_value, (1.0, -1.0)[side]
        flag = flags[edge : edge + 1, :] > 0
        rows[side, 0] = value
        rows[side, 1] = -sign * near
        rows[side, 2] = span(sign * value, -sign * near, flag)
        rows[side, 3] = jnp.broadcast_to(offsets[0, edge : edge + 1, :], (FIELDS, COLS))
        rows[side, 4] = jnp.broadcast_to(flags[edge : edge + 1, :], (FIELDS, COLS)).astype(jnp.float32)
    for piece in bring:
        piece.wait()


def edge_change(ref, side, beyond):
    outer = ref[side, 0] - beyond if side == 0 else beyond - ref[side, 0]
    return (span(outer, ref[side, 1], ref[side, 4] > 0) - ref[side, 2]) * ref[side, 3]


def remap_kernel(
    source_in, dest_in, target_in, far_row, near_row, far_col, near_col, start_x, cols, rows, own,
    flux, parts, mass, x, source, dest, target, tiles, marks, sems, count, input_sems,
):
    inputs = [
        pltpu.make_async_copy(held, here, input_sems.at[i])
        for i, (held, here) in enumerate(((source_in, source), (dest_in, dest), (target_in, target)))
    ]
    for copy in inputs:
        copy.start()

    def tile_copy(c):
        span_of = pl.ds(c * CHUNK, CHUNK)
        return pltpu.make_async_copy(flux.at[span_of], tiles.at[span_of], sems.at[c])

    for c in range(TILES // CHUNK):
        tile_copy(c).start()
    for side, beyond in enumerate(sides("sweep", near_row[:FIELDS, :], far_row[:FIELDS, :])):
        change = edge_change(rows, side, beyond)
        for h in range(2):
            at = pl.ds(((ROWS - 1) * side * 2 + h) * PAD, FIELDS)
            x[at, :] += change[:, h * BLK : (h + 1) * BLK]
    lanes = lane_of((ROWS, BLK))
    for side, beyond in enumerate(sides("cross", near_col[...], far_col[...])):
        change = edge_change(cols, side, beyond)
        for f in range(FIELDS):
            at = pl.ds(side * PAD + f, ROWS, stride=2 * PAD)
            x[at, :] += jnp.where(lanes == (BLK - 1) * side, change[:, f : f + 1], 0.0)
    marks[...] = jnp.full((SWEEPS, BLK), float(BLOCKS), jnp.float32)
    lanes = lane_of((1, BLK))

    def block(b):
        return x[pl.ds(pl.multiple_of(b * PAD, 8), PAD), :]

    def own_chunk(c, carry):
        first = c * CHUNK
        outs = [split_dot(block(first + k), own[first + k]) for k in range(CHUNK)]
        for k in range(CHUNK):
            mass[pl.ds(pl.multiple_of((first + k) * PAD, 8), PAD), :] = outs[k]
        return carry

    lax.fori_loop(0, BLOCKS // CHUNK, own_chunk, 0)
    for copy in inputs:
        copy.wait()
    for d in range(SWEEPS):
        count[d] = 0

    def flux_chunk(c, carry):
        tile_copy(c).wait()
        first = c * CHUNK
        outs = [split_dot(block(source[first + k]), tiles[first + k]) for k in range(CHUNK)]
        for k in range(CHUNK):
            d = dest[first + k]
            r = count[d]
            count[d] = r + 1
            parts[d, pl.ds(r * WIDE, WIDE), :] = outs[k][:WIDE]
            marks[pl.ds(d, 1), :] = jnp.where(
                lanes == r, target[first + k].astype(jnp.float32), marks[pl.ds(d, 1), :]
            )
        return carry

    lax.fori_loop(0, TILES // CHUNK, flux_chunk, 0)
    for d in range(SWEEPS):
        parts[d, pl.ds(SLOT_ROWS, 8), :] = jnp.broadcast_to(marks[d : d + 1, :], (8, BLK))


SUMS = 4
GROUP = 5
PIECES = 4
EARLY = 40


def receive_kernel(
    parts, mass, dense, far_row, near_row, far_col, near_col, found, where, sem, *totals
):
    for s in range(SWEEPS):
        found[s : s + 1, :] = parts[s, SLOT_ROWS : SLOT_ROWS + 1, :].astype(jnp.int32)
    naming = pltpu.make_async_copy(found, where, sem)
    naming.start()
    totals[0][pl.ds(0, BLOCKS * PAD), :] = mass[...]
    for total in totals[1:]:
        total[...] = jnp.zeros(total.shape, jnp.float32)
    naming.wait()
    for s in range(SWEEPS):
        for k in range(0, CAP, SUMS):
            at = [pl.ds(pl.multiple_of(where[s, k + j] * PAD, 8), PAD) for j in range(SUMS)]
            old = [totals[j][at[j], :] for j in range(SUMS)]
            for j in range(SUMS):
                totals[j][at[j], :] = old[j] + parts[s, (k + j) * WIDE : (k + j) * WIDE + PAD, :]

    for b in range(BLOCKS):
        at = pl.ds(b * PAD, PAD)
        value = sum(total[at, :] for total in totals)
        dense[at, :] = value * (1.0 / value[FIELDS:WIDE])

    def row(b):
        return jnp.concatenate(
            [dense[pl.ds((b + h) * PAD, FIELDS), :] for h in range(2)], axis=1
        )

    def col(h, lane):
        return packed(
            lambda f: dense[pl.ds(h * PAD + f, ROWS, stride=2 * PAD), :][:, lane : lane + 1]
        )

    pack_edges(
        row(0), row(BLOCKS - 2), col(0, 0), col(1, BLK - 1), far_row, near_row, far_col, near_col
    )


def inner_kernel(dense, out):
    for f in range(FIELDS):
        u = jnp.concatenate(
            [dense[pl.ds(h * PAD + f, ROWS, stride=2 * PAD), :] for h in range(2)], axis=1
        )
        up, down, left, right = bare(u)
        out[f] = u + SMOOTHING * (up + down + left + right - 4.0 * u)


def finish_kernel(inner, far_row, near_row, far_col, near_col, out, held, sems):
    low_row, high_row = sides("sweep", near_row[:FIELDS, :], far_row[:FIELDS, :])
    low_col, high_col = sides("cross", near_col[...], far_col[...])
    at_row, at_lane = row_of((ROWS, COLS)), lane_of((ROWS, COLS))
    copies = []
    for f in range(FIELDS):
        beyond = (
            jnp.where(at_row == 0, low_row[f : f + 1, :], 0.0)
            + jnp.where(at_row == ROWS - 1, high_row[f : f + 1, :], 0.0)
            + jnp.where(at_lane == 0, low_col[:, f : f + 1], 0.0)
            + jnp.where(at_lane == COLS - 1, high_col[:, f : f + 1], 0.0)
        )
        held[f] = inner[f] + SMOOTHING * beyond
        if f % GROUP == GROUP - 1:
            group = pl.ds(f + 1 - GROUP, GROUP)
            copies.append(
                pltpu.make_async_copy(held.at[group], out.at[group], sems.at[f // GROUP])
            )
            copies[-1].start()
    for copy in copies:
        copy.wait()


def in_place(held):
    return pltpu.with_memory_space_constraint(held, pltpu.HBM)


def params(mib):
    return pltpu.CompilerParams(vmem_limit_bytes=mib * 1024 * 1024)


def body(
    old_state, offsets, limiter_flags, self_tiles, flux_tiles, tile_source, tile_dest, tile_target
):
    vm, hbm = (pl.BlockSpec(memory_space=m) for m in (VMEM, pltpu.HBM))
    dma = pltpu.SemaphoreType.DMA
    shape = lambda *sizes: jax.ShapeDtypeStruct(sizes, jnp.float32)
    *edges, old, shifts, flags, own = pl.pallas_call(
        edges_kernel,
        out_shape=EDGES
        + (
            shape(FIELDS, ROWS, COLS), shape(2, ROWS, COLS),
            jax.ShapeDtypeStruct((ROWS, COLS), jnp.int32), shape(BLOCKS, BLK, BLK),
        ),
        in_specs=[hbm] * 4,
        out_specs=(vm,) * 8,
        scratch_shapes=[dma((FIELDS // GROUP + 3,))],
        compiler_params=params(16),
        name="edges",
    )(in_place(old_state), in_place(offsets), in_place(limiter_flags), in_place(self_tiles))
    halos = exchange(*edges)
    start_x, own, cols, rows = pl.pallas_call(
        stage_kernel,
        out_shape=(
            shape(BLOCKS * PAD, BLK), shape(BLOCKS, BLK, BLK),
            shape(2, 5, ROWS, BLK), shape(2, 5, FIELDS, COLS),
        ),
        in_specs=[vm] * 3 + [hbm, vm],
        out_specs=(vm,) * 4,
        input_output_aliases={4: 1},
        scratch_shapes=[dma((PIECES,))],
        compiler_params=params(16),
        cost_estimate=pl.CostEstimate(
            flops=40 * FIELDS * ROWS * COLS, bytes_accessed=BLOCKS * BLK * BLK * 4, transcendentals=0
        ),
        name="stage",
    )(old, shifts, flags, in_place(self_tiles), own)
    send, mass, _ = pl.pallas_call(
        remap_kernel,
        out_shape=(shape(SWEEPS, PART_ROWS, BLK), shape(BLOCKS * PAD, BLK), shape(BLOCKS * PAD, BLK)),
        in_specs=[hbm] * 3 + [vm] * 8 + [hbm],
        out_specs=(vm,) * 3,
        input_output_aliases={7: 2},
        scratch_shapes=[SMEM((TILES,), jnp.int32)] * 3
        + [
            VMEM((TILES, BLK, BLK), jnp.float32),
            VMEM((SWEEPS, BLK), jnp.float32),
            dma((TILES // CHUNK,)),
            SMEM((SWEEPS,), jnp.int32),
            dma((3,)),
        ],
        compiler_params=params(32),
        cost_estimate=pl.CostEstimate(
            flops=2 * 6 * (TILES + BLOCKS) * PAD * BLK * BLK,
            bytes_accessed=TILES * BLK * BLK * 4,
            transcendentals=0,
        ),
        name="remap",
    )(
        *(in_place(held) for held in (tile_source, tile_dest.reshape(TILES), tile_target)),
        *halos, start_x, cols, rows, own, in_place(flux_tiles),
    )
    arrived = lax.all_to_all(send, "sweep", split_axis=0, concat_axis=0, tiled=True)
    dense, *edges = pl.pallas_call(
        receive_kernel,
        out_shape=(shape(BLOCKS * PAD, BLK),) + EDGES,
        in_specs=[vm, vm],
        out_specs=(vm,) * 5,
        scratch_shapes=[VMEM((SWEEPS, BLK), jnp.int32), SMEM((SWEEPS, BLK), jnp.int32), dma]
        + [VMEM(((BLOCKS + 1) * PAD, BLK), jnp.float32)] * SUMS,
        compiler_params=params(32),
        name="receive",
    )(arrived, mass)
    halos = exchange(*edges)
    inner = pl.pallas_call(
        inner_kernel,
        out_shape=shape(FIELDS, ROWS, COLS),
        in_specs=[vm],
        out_specs=vm,
        compiler_params=params(16),
        cost_estimate=pl.CostEstimate(
            flops=20 * FIELDS * ROWS * COLS, bytes_accessed=8 * FIELDS * ROWS * COLS, transcendentals=0
        ),
        name="inner",
    )(dense)
    return pl.pallas_call(
        finish_kernel,
        out_shape=shape(FIELDS, ROWS, COLS),
        in_specs=[vm] * 5,
        out_specs=hbm,
        scratch_shapes=[VMEM((FIELDS, ROWS, COLS), jnp.float32), dma((FIELDS // GROUP,))],
        compiler_params=params(16),
        name="finish",
    )(inner, *halos)


def solution(mesh):
    placed = (
        P(None, "sweep", "cross"),
        P(None, "sweep", "cross"),
        P("sweep", "cross"),
        P(("sweep", "cross"), None, None),
        P(("sweep", "cross"), None, None),
        P(("sweep", "cross")),
        P(("sweep", "cross"), None),
        P(("sweep", "cross")),
    )
    return jax.shard_map(
        body, mesh=mesh, in_specs=placed, out_specs=P(None, "sweep", "cross"), check_vma=False
    )
```
